128 devices in a mesh: rep: 2 (over x_hi), dp: 8 (over y, core), tensor: 8 (over z, x_lo).
Axes of the slice: x: 4 (x_hi: 2, x_lo: 2; x = x_hi * 2 + x_lo), y: 4, z: 4, core: 2. Of those that a mesh axis runs over, the one named last changes fastest.
Arguments:
- hidden_in: bfloat16 [8192, 8192], P(('rep', 'dp')), may hold values from -6 to 6
- out_grad: bfloat16 [8192, 8192], P(('rep', 'dp'), 'tensor'), may hold values from -0.0059814453 to 0.0059814453
- queries: bfloat16 [8192, 8192], P(('rep', 'dp'), 'tensor'), may hold values from -120 to 120
- keys: bfloat16 [8192, 1024], P(('rep', 'dp'), 'tensor'), may hold values from -5 to 5
- segment_ids: int32 [16, 512], P(('rep', 'dp')), may hold values from 0 to 3, never falling along the last dimension, each value on 1 to 256 neighbouring positions
- value_codes: int32 [8192, 1024], P(('rep', 'dp'), 'tensor'), may hold values from 0 to 15
- value_steps: float32 [64, 1024], P(('rep', 'dp'), 'tensor'), may hold values from 0.0012 to 0.005
- output_codes: int32 [8192, 8192], P('tensor', ('rep', 'dp')), may hold values from 0 to 15
- output_steps: float32 [64, 8192], P('tensor', ('rep', 'dp')), may hold values from 0.0012 to 0.005
Outputs:
- output_step_grad: float32 [64, 8192], P('tensor', ('rep', 'dp'))
- value_step_grad: float32 [64, 1024], P(('rep', 'dp'), 'tensor')
- output_weight_grad: float32 [8192, 8192], P('tensor', ('rep', 'dp'))
- value_weight_grad: float32 [8192, 1024], P(('rep', 'dp'), 'tensor')
The draws below stay inside these ranges and needn't reach their ends.
All inputs are finite; a program needn't handle non-finite values.
Results may differ from the reference program's by a relative error of at most 0.02.
Values may be sent and summed in bfloat16 or wider, within the bound.
No kernel may reach another device: no remote copies, remote signals or barrier semaphores. Data moves between devices by JAX's collectives and lax.ppermute only.
A program may use at most 192 MiB of HBM per device.

```python
import math
import jax
import jax.numpy as jnp
import numpy as np
from jax import lax

D = 8192
HEADS = 64
KV_HEADS = 8
HD = 128
GROUP = 128
DOCS = 4
TOK_DEV = 512
GQ = 8
SEQS = 16
TOKENS = 8192


def shared_keys(key):
    return jnp.clip(jax.random.normal(key, (TOKENS, KV_HEADS * HD), jnp.float32), -5.0, 5.0)


def draw_keys(key, part):
    base = shared_keys(key)
    return base.astype(jnp.bfloat16)


def draw_queries(key, part):
    key = jax.random.fold_in(key, 5)
    return jnp.clip(jax.random.normal(key, (TOKENS, HEADS * HD), jnp.float32), -5.0, 5.0).astype(jnp.bfloat16)


def place_ends(result, stream_key, least, high):
    longest = result.shape.index(max(result.shape))
    spots = []
    for shift in (0, 1):
        where = [jax.random.randint(jax.random.fold_in(stream_key, axis), (), 0, length) for axis, length in enumerate(result.shape)]
        where[longest] = (where[longest] + shift) % result.shape[longest]
        spots.append(tuple(where))
    return result.at[spots[0]].set(least).at[spots[1]].set(high)


def level_of(own_key, extent, split, smallest, high):
    factor_of = 1.0
    for dim, shards_of in split:
        steps = jax.random.uniform(jax.random.fold_in(jax.random.fold_in(own_key, 6), dim), (shards_of,), jnp.float32, smallest / len(split), high / len(split))
        factor_of = factor_of * jnp.repeat(jnp.exp(steps), extent[dim] // shards_of).reshape((-1,) + (1,) * (len(extent) - 1 - dim))
    return factor_of


def split_up(number_of, total, most, skew):
    portions = [(1 << 20) // math.isqrt(standing ** skew) + 1 for standing in range(2, number_of + 1)]
    surplus, counts = total - most - (number_of - 1), [1] * (number_of - 1)
    while surplus > 0:
        free = [i for i in range(number_of - 1) if counts[i] < most]
        pool, left = sum([portions[i] for i in free]), surplus
        for i in free:
            extra = min(most - counts[i], max(1, left * portions[i] // pool), surplus)
            counts[i] = counts[i] + extra
            surplus = surplus - extra
    return np.array([most] + counts)


def ragged(own_key, count, total, limit, slope):
    if count == 2:
        one = jax.random.randint(own_key, (), max(1, total - limit), min(limit, total - 1) + 1)
        return jnp.stack([one, total - one])
    sizes = jnp.asarray(split_up(count, total, limit, slope), jnp.int32)
    couples = (count - 1) // 2
    donor, taker = sizes[1:1 + 2 * couples:2], sizes[2:2 + 2 * couples:2]
    margin = jnp.minimum(donor - 1, limit - taker)
    moved = jax.random.randint(jax.random.fold_in(own_key, 1), (couples,), 0, 1 << 20) % (margin + 1)
    sizes = sizes.at[1:1 + 2 * couples:2].set(donor - moved).at[2:2 + 2 * couples:2].set(taker + moved)
    return sizes[jax.random.permutation(jax.random.fold_in(own_key, 2), count)]


def scatter_about(rng, dims, spread, limit, split=(), held_as=jnp.bfloat16):
    drawn = jax.random.normal(rng, dims, jnp.float32) * spread
    if len(split) > 0:
        drawn = level_of(rng, dims, split, -0.22, 0.18) * drawn
    return jnp.clip(drawn, min=-limit, max=limit).astype(held_as)


def setup_inputs(seed: int = 0) -> dict:
    key_list = jax.random.split(jax.random.key(seed), 10)
    return {
        "hidden_in": scatter_about(key_list[0], (TOKENS, D), 1.0, 6.0, ((0, 16),)),
        "out_grad": scatter_about(key_list[1], (TOKENS, D), 0.001, 0.0059814453, ((0, 16), (1, 8))),
        "queries": draw_queries(jax.random.fold_in(key_list[9], 71), 0),
        "keys": draw_keys(jax.random.fold_in(key_list[9], 71), 0),
        "segment_ids": jax.vmap(lambda own: jnp.searchsorted(jnp.cumsum(ragged(own, DOCS, TOK_DEV, TOK_DEV // 2, 2)), jnp.arange(TOK_DEV), side="right"))(jax.random.split(key_list[4], SEQS)).reshape((SEQS, TOK_DEV)).astype(jnp.int32),
        "value_codes": place_ends(jax.random.randint(key_list[5], (D, KV_HEADS * HD), 0, 16), jax.random.fold_in(key_list[5], 1), 0, 15).astype(jnp.int32),
        "value_steps": jnp.clip(jnp.exp(math.log(0.005) - 1.4271163 * jax.random.uniform(key_list[6], (D // GROUP, KV_HEADS * HD), jnp.float32) ** level_of(key_list[6], (D // GROUP, KV_HEADS * HD), ((0, 16), (1, 8)), -0.2, 0.2)), 0.0012, 0.005),
        "output_codes": place_ends(jax.random.randint(key_list[7], (HEADS * HD, D), 0, 16), jax.random.fold_in(key_list[7], 1), 0, 15).astype(jnp.int32),
        "output_steps": jnp.clip(jnp.exp(math.log(0.005) - 1.4271163 * jax.random.uniform(key_list[8], (HEADS * HD // GROUP, D), jnp.float32) ** level_of(key_list[8], (HEADS * HD // GROUP, D), ((0, 8), (1, 16)), -0.2, 0.2)), 0.0012, 0.005),
    }


def dequant(codes, steps):
    full = jnp.repeat(steps, GROUP, axis=0)
    return (full * (codes - 8).astype(jnp.float32)).astype(jnp.bfloat16)


def attend(query_rows, key_rows, value_rows, segment_row):
    length = query_rows.shape[0]
    kv_local = key_rows.shape[1] // HD
    query_heads = query_rows.reshape(length, kv_local, GQ, HD).astype(jnp.float32)
    key_heads = key_rows.reshape(length, kv_local, HD).astype(jnp.float32)
    value_heads = value_rows.reshape(length, kv_local, HD).astype(jnp.float32)
    scores = jnp.einsum('ikgd,jkd->kgij', query_heads, key_heads) * (HD ** -0.5)
    position = jnp.arange(length)
    allowed = (position[None, :] <= position[:, None]) & (segment_row[:, None] == segment_row[None, :])
    scores = jnp.where(allowed[None, None], scores, -1e30)
    probs = jax.nn.softmax(scores, axis=-1).astype(jnp.bfloat16)
    attended = jnp.einsum('kgij,jkd->ikgd', probs.astype(jnp.float32), value_heads)
    return attended.astype(jnp.bfloat16).reshape(length, kv_local * GQ * HD), probs


def values_back(probs, attended_grad):
    length = attended_grad.shape[0]
    kv_local = probs.shape[0]
    grad_heads = attended_grad.reshape(length, kv_local, GQ, HD).astype(jnp.float32)
    back = jnp.einsum('kgij,ikgd->jkd', probs.astype(jnp.float32), grad_heads)
    return back.astype(jnp.bfloat16).reshape(length, kv_local * HD)


def reference(hidden_in, out_grad, queries, keys, segment_ids, value_codes, value_steps, output_codes, output_steps):
    value_weight = dequant(value_codes, value_steps)
    output_weight = dequant(output_codes, output_steps)

    def one_sequence(carry, index):
        acc_out, acc_value = carry
        start = (index * TOK_DEV).astype(jnp.int32)
        rows = lax.dynamic_slice_in_dim(hidden_in, start, TOK_DEV, 0)
        grads = lax.dynamic_slice_in_dim(out_grad, start, TOK_DEV, 0)
        query_rows = lax.dynamic_slice_in_dim(queries, start, TOK_DEV, 0)
        key_rows = lax.dynamic_slice_in_dim(keys, start, TOK_DEV, 0)
        values = jnp.dot(rows, value_weight, preferred_element_type=jnp.float32).astype(jnp.bfloat16)
        attended, probs = attend(query_rows, key_rows, values, segment_ids[index])
        attended_grad = jnp.dot(grads, output_weight.T, preferred_element_type=jnp.float32).astype(jnp.bfloat16)
        values_grad = values_back(probs, attended_grad)
        part_out = lax.optimization_barrier(jnp.dot(attended.T, grads, preferred_element_type=jnp.float32).astype(jnp.bfloat16))
        part_value = lax.optimization_barrier(jnp.dot(rows.T, values_grad, preferred_element_type=jnp.float32).astype(jnp.bfloat16))
        return (acc_out + part_out.astype(jnp.float32), acc_value + part_value.astype(jnp.float32)), None

    start_out = jnp.zeros((HEADS * HD, D), jnp.float32)
    start_value = jnp.zeros((D, KV_HEADS * HD), jnp.float32)
    (out_weight_grad, value_weight_grad), _ = lax.scan(one_sequence, (start_out, start_value), jnp.arange(SEQS, dtype=jnp.int32))
    output_step_grad = ((output_codes - 8).astype(jnp.float32) * out_weight_grad).reshape(HEADS * HD // GROUP, GROUP, D).sum(axis=1)
    value_step_grad = ((value_codes - 8).astype(jnp.float32) * value_weight_grad).reshape(D // GROUP, GROUP, KV_HEADS * HD).sum(axis=1)
    return output_step_grad, value_step_grad, out_weight_grad, value_weight_grad
```

```python
import jax
import jax.numpy as jnp
from jax import lax
from jax.sharding import Mesh, PartitionSpec as P

HD = 128
GROUP = 128
GQ = 8
SIZES = {"xh": 2, "y": 4, "c": 2, "z": 4, "xl": 2}
ROWS = ("xh", "y", "c")
HEADS_AXES = ("z", "xl")
F32 = jnp.float32
BF16 = jnp.bfloat16


def shift(x, axis, step):
    n = SIZES[axis]
    return lax.ppermute(x, axis, [(i, (i + step) % n) for i in range(n)])


def dequant(codes, steps):
    full = jnp.repeat(steps, GROUP, axis=0)
    return (full * (codes - 8).astype(F32)).astype(BF16)


def attention_probs(query_rows, key_rows, segment_row):
    length = query_rows.shape[0]
    query_heads = query_rows.reshape(length, GQ, HD)
    scores = jnp.einsum(
        "igd,jd->gij", query_heads, key_rows, preferred_element_type=F32
    ) * HD ** (-0.5)
    position = jnp.arange(length)
    allowed = (position[None, :] <= position[:, None]) & (
        segment_row[:, None] == segment_row[None, :]
    )
    scores = jnp.where(allowed[None], scores, -1e30)
    return jax.nn.softmax(scores, axis=-1).astype(BF16)


def pick(x, index):
    return lax.dynamic_index_in_dim(x, index, 0, keepdims=False)


def ordered(first, own, other):
    return jnp.stack([jnp.where(first, own, other), jnp.where(first, other, own)])


def gather_value_rows(piece, xh, y, c):
    pair = ordered(xh == 0, piece, shift(piece, "xh", 1))
    below, above = shift(pair, "y", 1), shift(pair, "y", -1)
    far = jnp.stack([shift(below[0], "y", 1), shift(above[1], "y", -1)])
    ring = jnp.stack([pair, above, far, below])
    ring = lax.dynamic_slice_in_dim(jnp.concatenate([ring, ring]), (4 - y) % 4, 4, 0)
    both = ordered(c == 0, ring, shift(ring, "c", 1))
    return both.transpose(2, 1, 0, 3, 4).reshape(-1, piece.shape[1])


def scatter_value_rows(term, xh, y, c):
    term = term.reshape(2, 4, 2, -1, term.shape[1]).transpose(2, 0, 1, 3, 4)
    mine = pick(term, c) + shift(pick(term, 1 - c).astype(BF16), "c", 1).astype(F32)
    mine = jnp.where(xh == 0, mine, mine[::-1])
    mine = lax.dynamic_slice_in_dim(jnp.concatenate([mine, mine], axis=1), y, 4, 1)
    low = shift(mine[0, 2].astype(BF16), "y", 1).astype(F32)
    high = shift(mine[1, 2].astype(BF16), "y", -1).astype(F32)
    up = shift(jnp.stack([mine[0, 1] + low, mine[1, 1]]).astype(BF16), "y", 1)
    down = shift(jnp.stack([mine[0, 3], mine[1, 3] + high]).astype(BF16), "y", -1)
    total = mine[:, 0] + up.astype(F32) + down.astype(F32)
    return total[0] + shift(total[1].astype(BF16), "xh", 1).astype(F32)


def ring_pieces(own, other, axis):
    pieces = {(0, 0): own, (0, 1): other}
    pieces[3, 0] = shift(own, axis, 1)
    pieces[1, 0] = shift(own, axis, -1)
    pieces[3, 1] = shift(other, axis, 1)
    pieces[1, 1] = shift(other, axis, -1)
    pieces[2, 0] = shift(pieces[3, 0], axis, 1)
    pieces[2, 1] = shift(pieces[1, 1], axis, -1)
    return pieces


def body(
    hidden_in,
    out_grad,
    queries,
    keys,
    segment_ids,
    value_codes,
    value_steps,
    output_codes,
    output_steps,
):
    xh, y, c, z, xl = (lax.axis_index(a) for a in SIZES)
    half = output_codes.shape[1]

    keep = lax.dynamic_slice_in_dim(out_grad, c * half, half, 1)
    give = lax.dynamic_slice_in_dim(out_grad, (1 - c) * half, half, 1)
    grads = jnp.concatenate([keep, shift(give, "c", 1)], axis=0)

    value_weight = gather_value_rows(dequant(value_codes, value_steps), xh, y, c)

    weight = dequant(output_codes, output_steps)
    weights = ring_pieces(weight, shift(weight, "xh", 1), "y")
    pieces = ring_pieces(grads, shift(grads, "xl", 1), "z")
    grads_all = jnp.zeros((8,) + grads.shape, BF16)
    for (distance, side), piece in pieces.items():
        where = ((z + distance) % 4) * 2 + (xl ^ side)
        grads_all = lax.dynamic_update_index_in_dim(grads_all, piece, where, 0)

    def grads_of(distance, side):
        return pick(grads_all, (xh ^ side) * 4 + (y + distance) % 4)

    probs = attention_probs(queries, keys, segment_ids[0])
    values = jnp.dot(hidden_in, value_weight, preferred_element_type=F32).astype(BF16)
    attended = jnp.einsum("gij,jd->igd", probs, values, preferred_element_type=F32)
    attended = attended.astype(BF16).reshape(values.shape[0], GQ * HD)
    attended = jnp.concatenate([attended, shift(attended, "c", 1)], axis=0)

    partial = 0.0
    for key, piece in weights.items():
        partial += lax.dot_general(
            grads_of(*key), piece, (((1,), (1,)), ((), ())), preferred_element_type=F32
        )
    length = values.shape[0]
    from_other = shift(partial[length:].astype(BF16), "c", 1)
    attended_grad = (partial[:length] + from_other.astype(F32)).astype(BF16)
    values_grad = jnp.einsum(
        "gij,igd->jd", probs, attended_grad.reshape(length, GQ, HD), preferred_element_type=F32
    ).astype(BF16)
    value_term = lax.dot_general(
        hidden_in, values_grad, (((0,), (0,)), ((), ())), preferred_element_type=F32
    )
    value_weight_grad = scatter_value_rows(value_term, xh, y, c)

    def part(distance, side):
        return lax.dot_general(
            attended, grads_of(distance, side), (((0,), (0,)), ((), ())), preferred_element_type=F32
        )

    low = shift(part(2, 0).astype(BF16), "y", 1).astype(F32)
    high = shift(part(2, 1).astype(BF16), "y", -1).astype(F32)
    up1 = shift(part(1, 1).astype(BF16), "y", 1).astype(F32)
    down1 = shift((part(3, 1) + high).astype(BF16), "y", -1).astype(F32)
    up0 = shift((part(1, 0) + low).astype(BF16), "y", 1).astype(F32)
    down0 = shift(part(3, 0).astype(BF16), "y", -1).astype(F32)
    across = shift((part(0, 1) + up1 + down1).astype(BF16), "xh", 1).astype(F32)
    output_weight_grad = part(0, 0) + up0 + down0 + across

    centered_out = (output_codes - 8).astype(F32)
    output_step_grad = (centered_out * output_weight_grad).reshape(-1, GROUP, half).sum(axis=1)
    centered_value = (value_codes - 8).astype(F32)
    value_step_grad = (
        (centered_value * value_weight_grad).reshape(-1, GROUP, value_codes.shape[1]).sum(axis=1)
    )
    return (output_step_grad, value_step_grad, output_weight_grad, value_weight_grad)


def solution(mesh):
    fine = Mesh(mesh.devices.reshape(tuple(SIZES.values())), tuple(SIZES))
    return jax.shard_map(
        body,
        mesh=fine,
        in_specs=(
            P(ROWS, None),
            P(ROWS, HEADS_AXES),
            P(ROWS, HEADS_AXES),
            P(ROWS, HEADS_AXES),
            P(ROWS, None),
            P(ROWS, HEADS_AXES),
            P(ROWS, HEADS_AXES),
            P(HEADS_AXES, ROWS),
            P(HEADS_AXES, ROWS),
        ),
        out_specs=(
            P(HEADS_AXES, ROWS),
            P(ROWS, HEADS_AXES),
            P(HEADS_AXES, ROWS),
            P(ROWS, HEADS_AXES),
        ),
        check_vma=False,
    )
```

```python
import jax
import jax.numpy as jnp
from jax import lax
from jax.experimental import pallas as pl
from jax.experimental.pallas import tpu as pltpu
from jax.sharding import Mesh, PartitionSpec as P

HD = 128
GROUP = 128
GQ = 8
SIZES = {"xh": 2, "y": 4, "c": 2, "z": 4, "xl": 2}
ROWS = ("xh", "y", "c")
HEADS_AXES = ("z", "xl")
F32 = jnp.float32
BF16 = jnp.bfloat16


def shift(x, axis, step):
    n = SIZES[axis]
    return lax.ppermute(x, axis, [(i, (i + step) % n) for i in range(n)])


def dequant(codes, steps):
    full = jnp.repeat(steps, GROUP, axis=0)
    return (full * (codes - 8).astype(F32)).astype(BF16)


def attention_probs(query_rows, key_rows, segment_row):
    length = query_rows.shape[0]
    query_heads = query_rows.reshape(length, GQ, HD)
    scores = jnp.einsum(
        "igd,jd->gij", query_heads, key_rows, preferred_element_type=F32
    ) * HD ** (-0.5)
    position = jnp.arange(length)
    allowed = (position[None, :] <= position[:, None]) & (
        segment_row[:, None] == segment_row[None, :]
    )
    scores = jnp.where(allowed[None], scores, -1e30)
    return jax.nn.softmax(scores, axis=-1).astype(BF16)


def pick(x, index):
    return lax.dynamic_index_in_dim(x, index, 0, keepdims=False)


def sum_of_blocks(hidden_in, mine, theirs, own_order, other_order):
    count, depth, columns = mine.shape
    rows = hidden_in.shape[0]

    def kernel(own_ref, other_ref, h_own, h_other, v_own, v_other, out, total):
        k = pl.program_id(0)

        @pl.when(k == 0)
        def _():
            total[...] = jnp.zeros_like(total)

        total[...] += jnp.dot(h_own[...], v_own[0], preferred_element_type=F32)
        total[...] += jnp.dot(h_other[...], v_other[0], preferred_element_type=F32)

        @pl.when(k == count - 1)
        def _():
            out[...] = total[...].astype(out.dtype)

    return pl.pallas_call(
        kernel,
        out_shape=jax.ShapeDtypeStruct((rows, columns), BF16),
        grid_spec=pltpu.PrefetchScalarGridSpec(
            num_scalar_prefetch=2,
            grid=(count,),
            in_specs=[
                pl.BlockSpec((rows, depth), lambda k, own, other: (0, own[k])),
                pl.BlockSpec((rows, depth), lambda k, own, other: (0, other[k])),
                pl.BlockSpec((1, depth, columns), lambda k, own, other: (k, 0, 0)),
                pl.BlockSpec((1, depth, columns), lambda k, own, other: (k, 0, 0)),
            ],
            out_specs=pl.BlockSpec((rows, columns), lambda k, own, other: (0, 0)),
            scratch_shapes=[pltpu.VMEM((rows, columns), F32)],
        ),
        compiler_params=pltpu.CompilerParams(vmem_limit_bytes=24 << 20),
        cost_estimate=pl.CostEstimate(
            flops=4 * count * rows * depth * columns, bytes_accessed=12 << 20, transcendentals=0
        ),
    )(own_order, other_order, hidden_in, hidden_in, mine, theirs)


def value_terms(hidden_in, grad, own_order, other_order):
    count = own_order.shape[0]
    columns, rows = grad.shape
    width = hidden_in.shape[1] // (2 * count)

    def kernel(own_ref, other_ref, h_own, h_other, grad_ref, own_out, other_out):
        own_out[0] = jnp.dot(grad_ref[...], h_own[...], preferred_element_type=F32)
        other = jnp.dot(grad_ref[...], h_other[...], preferred_element_type=F32)
        other_out[0] = other.astype(BF16)

    return pl.pallas_call(
        kernel,
        out_shape=(
            jax.ShapeDtypeStruct((count, columns, width), F32),
            jax.ShapeDtypeStruct((count, columns, width), BF16),
        ),
        grid_spec=pltpu.PrefetchScalarGridSpec(
            num_scalar_prefetch=2,
            grid=(count,),
            in_specs=[
                pl.BlockSpec((rows, width), lambda k, own, other: (0, own[k])),
                pl.BlockSpec((rows, width), lambda k, own, other: (0, other[k])),
                pl.BlockSpec((columns, rows), lambda k, own, other: (0, 0)),
            ],
            out_specs=(
                pl.BlockSpec((1, columns, width), lambda k, own, other: (k, 0, 0)),
                pl.BlockSpec((1, columns, width), lambda k, own, other: (k, 0, 0)),
            ),
        ),
        compiler_params=pltpu.CompilerParams(vmem_limit_bytes=24 << 20),
        cost_estimate=pl.CostEstimate(
            flops=4 * count * rows * width * columns, bytes_accessed=14 << 20, transcendentals=0
        ),
    )(own_order, other_order, hidden_in, hidden_in, grad)


def head_grads(grads_all, weights, order):
    count, rows, depth = grads_all.shape
    heads = weights[0].shape[0]
    tile = 256
    tiles = heads // tile
    half = rows // 2

    def kernel(order_ref, g_ref, *refs):
        w_refs, (own, other, held, total, sems) = refs[:count], refs[count:]
        k = pl.program_id(0)

        @pl.when(k == 0)
        def _():
            for i in range(count):
                pltpu.make_async_copy(w_refs[i], held.at[i], sems.at[i]).start()
            total[...] = jnp.zeros_like(total)

        pltpu.make_async_copy(w_refs[0], held.at[k], sems.at[k]).wait()

        def one(n, carry):
            block = held[k, pl.ds(pl.multiple_of(n * tile, tile), tile), :]
            total[n] += lax.dot_general(
                g_ref[0], block, (((1,), (1,)), ((), ())), preferred_element_type=F32
            )
            return carry

        lax.fori_loop(0, tiles, one, 0)

        @pl.when(k == count - 1)
        def _():
            for n in range(tiles):
                own[:, n * tile : (n + 1) * tile] = total[n, :half]
                other[:, n * tile : (n + 1) * tile] = total[n, half:].astype(BF16)

    return pl.pallas_call(
        kernel,
        out_shape=(
            jax.ShapeDtypeStruct((half, heads), F32),
            jax.ShapeDtypeStruct((half, heads), BF16),
        ),
        grid_spec=pltpu.PrefetchScalarGridSpec(
            num_scalar_prefetch=1,
            grid=(count,),
            in_specs=[pl.BlockSpec((1, rows, depth), lambda k, order: (order[k], 0, 0))]
            + [pl.BlockSpec(memory_space=pl.ANY)] * count,
            out_specs=(
                pl.BlockSpec((half, heads), lambda k, order: (0, 0)),
                pl.BlockSpec((half, heads), lambda k, order: (0, 0)),
            ),
            scratch_shapes=[
                pltpu.VMEM((count, heads, depth), BF16),
                pltpu.VMEM((tiles, rows, tile), F32),
                pltpu.SemaphoreType.DMA((count,)),
            ],
        ),
        compiler_params=pltpu.CompilerParams(vmem_limit_bytes=36 << 20),
        cost_estimate=pl.CostEstimate(
            flops=2 * count * rows * depth * heads, bytes_accessed=19 << 20, transcendentals=0
        ),
    )(order, grads_all, *weights)


def gate(arrays, *after):
    flat, tree = jax.tree.flatten((arrays, after))
    return jax.tree.unflatten(tree, lax.optimization_barrier(flat))[0]


def body(
    hidden_in,
    out_grad,
    queries,
    keys,
    segment_ids,
    value_codes,
    value_steps,
    output_codes,
    output_steps,
):
    xh, y, c, z, xl = (lax.axis_index(a) for a in SIZES)
    half = output_codes.shape[1]

    others = [(distance, side) for distance in range(4) for side in (0, 1)]

    def chip_at(distance, side):
        return (xh ^ side) * 4 + (y + distance) % 4

    chips = jnp.stack([chip_at(*key) for key in others]).astype(jnp.int32)
    own_order, other_order = chips * 2 + c, chips * 2 + 1 - c

    keep = lax.dynamic_slice_in_dim(out_grad, c * half, half, 1)
    give = lax.dynamic_slice_in_dim(out_grad, (1 - c) * half, half, 1)
    grads = jnp.concatenate([keep, shift(give, "c", 1)], axis=0)
    rows = dequant(value_codes, value_steps)
    rows = jnp.stack([rows, shift(rows, "xh", 1)])
    weight = dequant(output_codes, output_steps)
    grads, rows, weight, queries = gate((grads, rows, weight, queries))

    g, w, v = {(0, 0): grads}, {(0, 0): weight}, {0: rows}
    w[3, 0], w[1, 0] = shift(weight, "y", 1), shift(weight, "y", -1)
    g[3, 0], g[1, 0] = shift(grads, "z", 1), shift(grads, "z", -1)
    g[0, 1] = shift(grads, "xl", 1)
    v[3], v[1] = shift(rows, "y", 1), shift(rows, "y", -1)
    probs = attention_probs(queries, keys, segment_ids[0])
    g, w, v, probs = gate((g, w, v, probs))

    cut = weight.shape[0] // 2
    g[3, 1], g[1, 1] = shift(g[0, 1], "z", 1), shift(g[0, 1], "z", -1)
    w[0, 1] = shift(weight, "xh", 1)
    v_far = shift(v[3][0], "y", 1), shift(v[1][1], "y", -1)
    far = [shift(w[3, 0][:cut], "y", 1), shift(w[1, 0][cut:], "y", -1)]

    def place(grads_all, keys_of):
        for key in keys_of:
            where = ((z + key[0]) % 4) * 2 + (xl ^ key[1])
            grads_all = lax.dynamic_update_index_in_dim(grads_all, g[key], where, 0)
        return grads_all

    grads_all = place(jnp.zeros((8,) + grads.shape, BF16), [(0, 0), (1, 0), (3, 0), (0, 1)])
    g, w, v, far, v_far, grads_all = gate((g, w, v, far, v_far, grads_all))

    w[2, 0] = jnp.concatenate(far, axis=0)
    w[3, 1], w[1, 1] = shift(w[0, 1], "y", 1), shift(w[0, 1], "y", -1)
    w[2, 1] = shift(w[2, 0], "xh", 1)
    g[2, 0], g[2, 1] = shift(g[3, 0], "z", 1), shift(g[1, 1], "z", -1)
    grads_all = place(grads_all, [(1, 1), (3, 1)])
    mine = jnp.concatenate([v[0], v[1], v_far[0][None], v_far[1][None], v[3]])
    values = sum_of_blocks(hidden_in, mine, shift(mine, "c", 1), own_order, other_order)
    attended = jnp.einsum("gij,jd->igd", probs, values, preferred_element_type=F32)
    attended = attended.astype(BF16).reshape(values.shape[0], GQ * HD)
    attended = jnp.concatenate([attended, shift(attended, "c", 1)], axis=0)
    g, w, attended, grads_all, probs = gate((g, w, attended, grads_all, probs))
    grads_all = place(grads_all, [(2, 0), (2, 1)])

    def part(distance, side):
        block = pick(grads_all, chip_at(distance, side))
        return lax.dot_general(
            attended, block, (((0,), (0,)), ((), ())), preferred_element_type=F32
        )

    up1 = part(1, 1).astype(BF16)
    down1 = part(3, 1).astype(BF16)
    cross = part(2, 1).astype(BF16)
    up1, down1, cross, grads_all = gate((up1, down1, cross, grads_all))
    up1, down1, cross = shift(up1, "y", 1), shift(down1, "y", -1), shift(cross, "xh", 1)

    length = values.shape[0]
    here, there = head_grads(grads_all, [w[key] for key in others], chips)
    attended_grad = (here + shift(there, "c", 1).astype(F32)).astype(BF16)
    values_grad = jnp.einsum(
        "gij,igd->dj", probs, attended_grad.reshape(length, GQ, HD), preferred_element_type=F32
    ).astype(BF16)
    values_grad, up1, down1, cross, grads_all = gate((values_grad, up1, down1, cross, grads_all))

    far_part = (part(2, 0) + cross.astype(F32)).astype(BF16)
    low = shift(far_part[:cut], "y", 1)
    high = shift(far_part[cut:], "y", -1)
    across = part(0, 1) + up1.astype(F32) + down1.astype(F32)
    across = shift(across.astype(BF16), "xh", 1)
    up_part, down_part = part(1, 0), part(3, 0)
    term, term_give = value_terms(hidden_in, values_grad, own_order, other_order)
    term = term + shift(term_give, "c", 1).astype(F32)
    term_low = shift(term[4].astype(BF16), "y", 1)
    term_high = shift(term[5].astype(BF16), "y", -1)
    low, high, across, up_part, down_part, term, term_low, term_high, grads_all = gate(
        (low, high, across, up_part, down_part, term, term_low, term_high, grads_all)
    )

    term_up = jnp.stack([term[2] + term_low.astype(F32), term[3]]).astype(BF16)
    term_down = jnp.stack([term[6], term[7] + term_high.astype(F32)]).astype(BF16)
    term_up, term_down = shift(term_up, "y", 1), shift(term_down, "y", -1)
    up0 = jnp.concatenate([up_part[:cut] + low.astype(F32), up_part[cut:]], axis=0)
    down0 = jnp.concatenate([down_part[:cut], down_part[cut:] + high.astype(F32)], axis=0)
    up0 = shift(up0.astype(BF16), "y", 1)
    down0 = shift(down0.astype(BF16), "y", -1)
    term = term[:2] + term_up.astype(F32) + term_down.astype(F32)
    term = term[0] + shift(term[1].astype(BF16), "xh", 1).astype(F32)
    value_weight_grad = term.T
    output_weight_grad = part(0, 0) + across.astype(F32) + up0.astype(F32) + down0.astype(F32)

    centered_out = (output_codes - 8).astype(F32)
    output_step_grad = (centered_out * output_weight_grad).reshape(-1, GROUP, half).sum(axis=1)
    centered_value = (value_codes - 8).astype(F32)
    value_step_grad = (
        (centered_value * value_weight_grad).reshape(-1, GROUP, value_codes.shape[1]).sum(axis=1)
    )
    return (output_step_grad, value_step_grad, output_weight_grad, value_weight_grad)


def solution(mesh):
    fine = Mesh(mesh.devices.reshape(tuple(SIZES.values())), tuple(SIZES))
    return jax.shard_map(
        body,
        mesh=fine,
        in_specs=(
            P(ROWS, None),
            P(ROWS, HEADS_AXES),
            P(ROWS, HEADS_AXES),
            P(ROWS, HEADS_AXES),
            P(ROWS, None),
            P(ROWS, HEADS_AXES),
            P(ROWS, HEADS_AXES),
            P(HEADS_AXES, ROWS),
            P(HEADS_AXES, ROWS),
        ),
        out_specs=(
            P(HEADS_AXES, ROWS),
            P(ROWS, HEADS_AXES),
            P(HEADS_AXES, ROWS),
            P(ROWS, HEADS_AXES),
        ),
        check_vma=False,
    )
```

```python
import jax
import jax.numpy as jnp
from jax import lax
from jax.experimental import pallas as pl
from jax.experimental.pallas import tpu as pltpu
from jax.sharding import Mesh, PartitionSpec as P

HD = 128
GROUP = 128
GQ = 8
SIZES = {"xh": 2, "y": 4, "c": 2, "z": 4, "xl": 2}
ROWS = ("xh", "y", "c")
HEADS_AXES = ("z", "xl")
F32 = jnp.float32
BF16 = jnp.bfloat16
TOGETHER = 2
LONG = pl.CostEstimate(flops=1 << 35, bytes_accessed=1 << 24, transcendentals=0)
BRIEF = pl.CostEstimate(flops=1 << 20, bytes_accessed=1 << 16, transcendentals=0)


def shift(x, axis, step):
    n = SIZES[axis]
    return lax.ppermute(x, axis, [(i, (i + step) % n) for i in range(n)])


def dequant_rows(codes, steps):
    rows, columns = codes.shape

    def kernel(codes_ref, steps_ref, out):
        for k in range(rows // GROUP):
            group = slice(k * GROUP, (k + 1) * GROUP)
            centered = (codes_ref[group, :] - 8).astype(F32)
            out[group, :] = (centered * steps_ref[k : k + 1, :]).astype(BF16)

    return pl.pallas_call(
        kernel,
        out_shape=jax.ShapeDtypeStruct((rows, columns), BF16),
        cost_estimate=BRIEF,
    )(codes, steps)


def dequant_transposed(codes, steps):
    rows, columns = codes.shape
    block = rows // 2
    groups = block // GROUP

    def kernel(codes_ref, steps_ref, out):
        for k in range(groups):
            group = slice(k * GROUP, (k + 1) * GROUP)
            centered = (codes_ref[group, :] - 8).astype(F32)
            step = steps_ref[pl.ds(pl.program_id(0) * groups + k, 1), :]
            out[:, group] = (centered * step).astype(BF16).T

    return pl.pallas_call(
        kernel,
        out_shape=jax.ShapeDtypeStruct((columns, rows), BF16),
        grid=(rows // block,),
        in_specs=[
            pl.BlockSpec((block, columns), lambda k: (k, 0)),
            pl.BlockSpec(steps.shape, lambda k: (0, 0)),
        ],
        out_specs=pl.BlockSpec((columns, block), lambda k: (0, k)),
        cost_estimate=BRIEF,
    )(codes, steps)


def attention_probs(queries, keys, segment_ids, first, count):
    length = keys.shape[0]

    def kernel(q_ref, k_ref, down_ref, along_ref, out, allowed):
        @pl.when(pl.program_id(0) == 0)
        def _():
            key_at = lax.broadcasted_iota(jnp.int32, (length, length), 0)
            query_at = lax.broadcasted_iota(jnp.int32, (length, length), 1)
            seen = (key_at <= query_at) & (down_ref[...] == along_ref[...])
            allowed[...] = seen.astype(F32)

        scores = lax.dot_general(
            k_ref[...], q_ref[...], (((1,), (1,)), ((), ())), preferred_element_type=F32
        ) * HD ** (-0.5)
        scores = jnp.where(allowed[...] > 0.5, scores, -1e30)
        powers = jnp.exp(scores - jnp.max(scores, axis=0, keepdims=True))
        out[0] = (powers / jnp.sum(powers, axis=0, keepdims=True)).astype(BF16)

    return pl.pallas_call(
        kernel,
        out_shape=jax.ShapeDtypeStruct((count, length, length), BF16),
        grid=(count,),
        in_specs=[
            pl.BlockSpec((length, HD), lambda h: (0, first + h)),
            pl.BlockSpec((length, HD), lambda h: (0, 0)),
            pl.BlockSpec((length, 1), lambda h: (0, 0)),
            pl.BlockSpec((1, length), lambda h: (0, 0)),
        ],
        out_specs=pl.BlockSpec((1, length, length), lambda h: (h, 0, 0)),
        scratch_shapes=[pltpu.VMEM((length, length), F32)],
        compiler_params=pltpu.CompilerParams(vmem_limit_bytes=32 << 20),
        cost_estimate=LONG,
    )(queries, keys, segment_ids.reshape(length, 1), segment_ids)


def attended_heads(hidden_in, value_weight, probs):
    width, columns = value_weight.shape
    rows = hidden_in.shape[0]
    heads = 2 * probs[0].shape[0]
    count = 8
    depth = width // count

    def kernel(h_ref, v_ref, p_low, p_high, out, total):
        k = pl.program_id(0)
        more = jnp.dot(h_ref[...], v_ref[...], preferred_element_type=F32)

        @pl.when(k == 0)
        def _():
            total[...] = more

        @pl.when(k > 0)
        def _():
            total[...] += more

        @pl.when(k == count - 1)
        def _():
            values = total[...].T.astype(BF16)
            for h in range(heads):
                p_ref = (p_low, p_high)[h // (heads // 2)]
                one = jnp.dot(values, p_ref[h % (heads // 2)], preferred_element_type=F32)
                out[h * columns : (h + 1) * columns, :] = one.astype(BF16)

    whole = pl.BlockSpec(probs[0].shape, lambda k: (0, 0, 0))
    return pl.pallas_call(
        kernel,
        out_shape=jax.ShapeDtypeStruct((heads * columns, rows), BF16),
        grid=(count,),
        in_specs=[
            pl.BlockSpec((rows, depth), lambda k: (0, k)),
            pl.BlockSpec((depth, columns), lambda k: (k, 0)),
            whole,
            whole,
        ],
        out_specs=pl.BlockSpec((heads * columns, rows), lambda k: (0, 0)),
        scratch_shapes=[pltpu.VMEM((rows, columns), F32)],
        compiler_params=pltpu.CompilerParams(vmem_limit_bytes=56 << 20),
        cost_estimate=LONG,
    )(hidden_in, value_weight, *probs)


def value_terms(hidden_in, here, there, probs, own_order, other_order):
    count = own_order.shape[0]
    rows, heads = here.shape
    width = hidden_in.shape[1] // (2 * count)
    half = probs[0].shape[0]

    def kernel(own_ref, other_ref, h_own, h_other, a_ref, b_ref, p_low, p_high, *refs):
        own_out, other_out, grad = refs

        @pl.when(pl.program_id(0) == 0)
        def _():
            total = jnp.zeros((rows, HD), F32)
            for h in range(2 * half):
                head = slice(h * HD, (h + 1) * HD)
                attended_grad = (a_ref[:, head] + b_ref[:, head].astype(F32)).astype(BF16)
                p_ref = (p_low, p_high)[h // half]
                total += jnp.dot(p_ref[h % half], attended_grad, preferred_element_type=F32)
            grad[...] = total.T.astype(BF16)

        own_out[0] = jnp.dot(grad[...], h_own[...], preferred_element_type=F32)
        other = jnp.dot(grad[...], h_other[...], preferred_element_type=F32)
        other_out[0] = other.astype(BF16)

    whole = pl.BlockSpec(probs[0].shape, lambda k, own, other: (0, 0, 0))
    return pl.pallas_call(
        kernel,
        out_shape=(
            jax.ShapeDtypeStruct((count, HD, width), F32),
            jax.ShapeDtypeStruct((count, HD, width), BF16),
        ),
        grid_spec=pltpu.PrefetchScalarGridSpec(
            num_scalar_prefetch=2,
            grid=(count,),
            in_specs=[
                pl.BlockSpec((rows, width), lambda k, own, other: (0, own[k])),
                pl.BlockSpec((rows, width), lambda k, own, other: (0, other[k])),
                pl.BlockSpec((rows, heads), lambda k, own, other: (0, 0)),
                pl.BlockSpec((rows, heads), lambda k, own, other: (0, 0)),
                whole,
                whole,
            ],
            out_specs=(
                pl.BlockSpec((1, HD, width), lambda k, own, other: (k, 0, 0)),
                pl.BlockSpec((1, HD, width), lambda k, own, other: (k, 0, 0)),
            ),
            scratch_shapes=[pltpu.VMEM((HD, rows), BF16)],
        ),
        compiler_params=pltpu.CompilerParams(vmem_limit_bytes=56 << 20),
        cost_estimate=BRIEF,
    )(own_order, other_order, hidden_in, hidden_in, here, there, *probs)


def value_grads(own, others, codes):
    columns, rows = own.shape

    def kernel(own_ref, *refs):
        refs, (codes_ref, step_out, out) = refs[: len(others)], refs[len(others) :]
        total = own_ref[...]
        for ref in refs:
            total += ref[...].astype(F32)
        total = total.T
        out[...] = total
        centered = (codes_ref[...] - 8).astype(F32) * total
        for k in range(rows // GROUP):
            group = centered[k * GROUP : (k + 1) * GROUP]
            step_out[k : k + 1, :] = jnp.sum(group, axis=0, keepdims=True)

    return pl.pallas_call(
        kernel,
        out_shape=(
            jax.ShapeDtypeStruct((rows // GROUP, columns), F32),
            jax.ShapeDtypeStruct((rows, columns), F32),
        ),
        cost_estimate=BRIEF,
    )(own, *others, codes)


def fetch_piece(which, pieces, target, sem):
    for i, piece in enumerate(pieces):

        @pl.when(which == i)
        def _():
            pltpu.make_async_copy(piece, target, sem).start()


def head_grads(grads, weights, order):
    count = len(weights)
    rows, depth = grads[0].shape
    heads = weights[0].shape[1]
    half = rows // 2
    steps = count // TOGETHER
    span = depth * TOGETHER

    def kernel(order_ref, *refs):
        g_refs, w_refs, refs = refs[:count], refs[count : 2 * count], refs[2 * count :]
        own, other, g_held, w_held, total, g_sems, w_sems = refs
        k = pl.program_id(0)

        def blocks(step):
            for i in range(TOGETHER):
                at = slice(i * depth, (i + 1) * depth)
                yield step * TOGETHER + i, g_held.at[step, :, at], w_held.at[step, at, :]

        @pl.when(k == 0)
        def _():
            for step in range(steps):
                for i, g_at, w_at in blocks(step):
                    fetch_piece(order_ref[i], g_refs, g_at, g_sems.at[step])
                    pltpu.make_async_copy(w_refs[i], w_at, w_sems.at[step]).start()
            total[...] = jnp.zeros_like(total)

        pltpu.make_async_copy(g_held.at[k], g_held.at[k], g_sems.at[k]).wait()
        pltpu.make_async_copy(w_held.at[k], w_held.at[k], w_sems.at[k]).wait()
        total[...] += jnp.dot(g_held[k], w_held[k], preferred_element_type=F32)

        @pl.when(k == steps - 1)
        def _():
            own[...] = total[:half]
            other[...] = total[half:].astype(BF16)

    return pl.pallas_call(
        kernel,
        out_shape=(
            jax.ShapeDtypeStruct((half, heads), F32),
            jax.ShapeDtypeStruct((half, heads), BF16),
        ),
        grid_spec=pltpu.PrefetchScalarGridSpec(
            num_scalar_prefetch=1,
            grid=(steps,),
            in_specs=[pl.BlockSpec(memory_space=pl.ANY)] * (2 * count),
            out_specs=(
                pl.BlockSpec((half, heads), lambda k, order: (0, 0)),
                pl.BlockSpec((half, heads), lambda k, order: (0, 0)),
            ),
            scratch_shapes=[
                pltpu.VMEM((steps, rows, span), BF16),
                pltpu.VMEM((steps, span, heads), BF16),
                pltpu.VMEM((rows, heads), F32),
                pltpu.SemaphoreType.DMA((steps,)),
                pltpu.SemaphoreType.DMA((steps,)),
            ],
        ),
        compiler_params=pltpu.CompilerParams(vmem_limit_bytes=52 << 20),
        cost_estimate=BRIEF,
    )(order, *grads, *weights)


def weight_parts(attended, grads, order):
    (count,) = order.shape
    rows, depth = grads[0].shape
    heads, half = attended[0].shape
    tile = 256

    def kernel(order_ref, first, second, *refs):
        g_refs, outs, refs = refs[: len(grads)], refs[len(grads) : -6], refs[-6:]
        a_held, held, done, a_sem, sems, out_sems = refs
        a_copies = [
            pltpu.make_async_copy(first, a_held.at[:, :half], a_sem.at[0]),
            pltpu.make_async_copy(second, a_held.at[:, half:], a_sem.at[1]),
        ]
        for copy in a_copies:
            copy.start()
        for k in range(count):
            fetch_piece(order_ref[k], g_refs, held.at[k], sems.at[k])
        for copy in a_copies:
            copy.wait()
        out_copies = []
        for k in range(count):
            pltpu.make_async_copy(g_refs[0], held.at[k], sems.at[k]).wait()
            for n in range(0, depth, tile):
                block = held[k, :, n : n + tile]
                one = jnp.dot(a_held[...], block, preferred_element_type=F32)
                done[k, :, n : n + tile] = one.astype(BF16)
            out_copies.append(pltpu.make_async_copy(done.at[k], outs[k], out_sems.at[k]))
            out_copies[-1].start()
        for copy in out_copies:
            copy.wait()

    anywhere = pl.BlockSpec(memory_space=pl.ANY)
    return pl.pallas_call(
        kernel,
        out_shape=(jax.ShapeDtypeStruct((heads, depth), BF16),) * count,
        grid_spec=pltpu.PrefetchScalarGridSpec(
            num_scalar_prefetch=1,
            in_specs=[anywhere] * (2 + len(grads)),
            out_specs=(anywhere,) * count,
            scratch_shapes=[
                pltpu.VMEM((heads, rows), BF16),
                pltpu.VMEM((count, rows, depth), BF16),
                pltpu.VMEM((count, heads, depth), BF16),
                pltpu.SemaphoreType.DMA((2,)),
                pltpu.SemaphoreType.DMA((count,)),
                pltpu.SemaphoreType.DMA((count,)),
            ],
        ),
        compiler_params=pltpu.CompilerParams(vmem_limit_bytes=48 << 20),
        cost_estimate=BRIEF,
    )(order, *attended, *grads)


def gate(arrays, *after):
    flat, tree = jax.tree.flatten((arrays, after))
    return jax.tree.unflatten(tree, lax.optimization_barrier(flat))[0]


def body(
    hidden_in,
    out_grad,
    queries,
    keys,
    segment_ids,
    value_codes,
    value_steps,
    output_codes,
    output_steps,
):
    xh, y, c, z, xl = (lax.axis_index(a) for a in SIZES)
    heads, half = output_codes.shape

    others = [(distance, side) for distance in range(4) for side in (0, 1)]

    def chip_at(distance, side):
        return (xh ^ side) * 4 + (y + distance) % 4

    chips = jnp.stack([chip_at(*key) for key in others]).astype(jnp.int32)
    own_order, other_order = chips * 2 + c, chips * 2 + 1 - c

    def piece_at(distance, side):
        chip = chip_at(distance, side)
        return ((chip // 2 - z) % 4) * 2 + ((chip % 2) ^ xl)

    def pieces_at(keys_of):
        return jnp.stack([piece_at(*key) for key in keys_of]).astype(jnp.int32)

    value_weight = lax.all_gather(dequant_rows(value_codes, value_steps), ROWS, axis=0, tiled=True)
    keep = lax.dynamic_slice_in_dim(out_grad, c * half, half, 1)
    give = lax.dynamic_slice_in_dim(out_grad, (1 - c) * half, half, 1)
    grads = jnp.concatenate([keep, shift(give, "c", 1)], axis=0)
    weight = dequant_transposed(output_codes, output_steps)
    grads, weight, queries = gate((grads, weight, queries))

    g, w = {(0, 0): grads}, {(0, 0): weight}
    w[3, 0], w[1, 0] = shift(weight, "y", 1), shift(weight, "y", -1)
    g[3, 0], g[1, 0] = shift(grads, "z", 1), shift(grads, "z", -1)
    g[0, 1] = shift(grads, "xl", 1)
    probs = [attention_probs(queries, keys, segment_ids, h, GQ // 2) for h in (0, GQ // 2)]
    g, w, probs = gate((g, w, probs))

    g[3, 1], g[1, 1] = shift(g[0, 1], "z", 1), shift(g[0, 1], "z", -1)
    w[0, 1] = shift(weight, "xh", 1)
    w[2, 0] = shift(w[3, 0], "y", 1)
    g, w, value_weight, probs = gate((g, w, value_weight, probs))

    w[3, 1], w[1, 1] = shift(w[0, 1], "y", 1), shift(w[0, 1], "y", -1)
    w[2, 1] = shift(w[2, 0], "xh", 1)
    g[2, 0], g[2, 1] = shift(g[3, 0], "z", 1), shift(g[1, 1], "z", -1)
    attended = attended_heads(hidden_in, value_weight, probs)
    g, w, attended, probs = gate((g, w, attended, probs))

    attended = attended, shift(attended, "c", 1)
    pieces = [g[key] for key in others]
    here, there = head_grads(pieces, [w[key] for key in others], pieces_at(others))
    here, there, pieces, attended = gate((here, there, pieces, attended))
    there = shift(there, "c", 1)
    up1, down1, cross = weight_parts(attended, pieces, pieces_at([(1, 1), (3, 1), (2, 1)]))
    here, there, up1, down1, cross = gate((here, there, up1, down1, cross))
    up1, down1, cross = shift(up1, "y", 1), shift(down1, "y", -1), shift(cross, "xh", 1)
    term, term_give = value_terms(hidden_in, here, there, probs, own_order, other_order)
    term, term_give, attended, pieces = gate((term, term_give, attended, pieces))
    far_part, across, up_part, down_part, stay = weight_parts(
        attended, pieces, pieces_at([(2, 0), (0, 1), (1, 0), (3, 0), (0, 0)])
    )
    term, term_give, up1, down1, cross, far_part, across, up_part, down_part, stay = gate(
        (term, term_give, up1, down1, cross, far_part, across, up_part, down_part, stay)
    )

    term = (term + shift(term_give, "c", 1).astype(F32)).reshape(4, 2, HD, half)
    term, term_give = term[:, 0], shift(term[:, 1].astype(BF16), "xh", 1)
    far_part = (far_part.astype(F32) + cross.astype(F32)).astype(BF16)
    low = shift(far_part[: heads // 2], "y", 1)
    high = shift(far_part[heads // 2 :], "y", -1)
    across = (across.astype(F32) + up1.astype(F32) + down1.astype(F32)).astype(BF16)
    low, high, across, up_part, down_part, stay, term, term_give = gate(
        (low, high, across, up_part, down_part, stay, term, term_give)
    )

    across = shift(across, "xh", 1)
    term = term + term_give.astype(F32)
    send = term.astype(BF16)
    low, high = low.astype(F32), high.astype(F32)
    up0, down0 = up_part.astype(F32), down_part.astype(F32)
    up0 = jnp.concatenate(
        [(up0[: heads // 2] + low).astype(BF16), up_part[heads // 2 :], send[1]], axis=0
    )
    down0 = jnp.concatenate(
        [down_part[: heads // 2], (down0[heads // 2 :] + high).astype(BF16), send[3]], axis=0
    )
    up0, down0 = shift(up0, "y", 1), shift(down0, "y", -1)
    term_far = shift(send[2], "y", 2)
    terms = (up0[heads:], down0[heads:], term_far)
    value_step_grad, value_weight_grad = value_grads(term[0], terms, value_codes)
    output_weight_grad = stay.astype(F32) + across.astype(F32)
    output_weight_grad += up0[:heads].astype(F32) + down0[:heads].astype(F32)
    centered_out = (output_codes - 8).astype(F32)
    output_step_grad = (centered_out * output_weight_grad).reshape(-1, GROUP, half).sum(axis=1)
    return (output_step_grad, value_step_grad, output_weight_grad, value_weight_grad)


def solution(mesh):
    fine = Mesh(mesh.devices.reshape(tuple(SIZES.values())), tuple(SIZES))
    return jax.shard_map(
        body,
        mesh=fine,
        in_specs=(
            P(ROWS, None),
            P(ROWS, HEADS_AXES),
            P(ROWS, HEADS_AXES),
            P(ROWS, HEADS_AXES),
            P(ROWS, None),
            P(ROWS, HEADS_AXES),
            P(ROWS, HEADS_AXES),
            P(HEADS_AXES, ROWS),
            P(HEADS_AXES, ROWS),
        ),
        out_specs=(
            P(HEADS_AXES, ROWS),
            P(ROWS, HEADS_AXES),
            P(HEADS_AXES, ROWS),
            P(ROWS, HEADS_AXES),
        ),
        check_vma=False,
    )
```

```python
import jax
import jax.numpy as jnp
from jax import lax
from jax.experimental import pallas as pl
from jax.experimental.pallas import tpu as pltpu
from jax.sharding import Mesh, PartitionSpec as P

HD = 128
GROUP = 128
GQ = 8
SIZES = {"xh": 2, "y": 4, "c": 2, "z": 4, "xl": 2}
ROWS = ("xh", "y", "c")
HEADS_AXES = ("z", "xl")
F32 = jnp.float32
BF16 = jnp.bfloat16
LONG = pl.CostEstimate(flops=1 << 35, bytes_accessed=1 << 24, transcendentals=0)
BRIEF = pl.CostEstimate(flops=1 << 20, bytes_accessed=1 << 16, transcendentals=0)


def shift(x, axis, step):
    n = SIZES[axis]
    return lax.ppermute(x, axis, [(i, (i + step) % n) for i in range(n)])


def dequant_rows(codes, steps):
    rows, columns = codes.shape

    def kernel(codes_ref, steps_ref, out):
        for k in range(rows // GROUP):
            group = slice(k * GROUP, (k + 1) * GROUP)
            centered = (codes_ref[group, :] - 8).astype(F32)
            out[group, :] = (centered * steps_ref[k : k + 1, :]).astype(BF16)

    return pl.pallas_call(
        kernel,
        out_shape=jax.ShapeDtypeStruct((rows, columns), BF16),
        cost_estimate=BRIEF,
    )(codes, steps)


def dequant_transposed(codes, steps):
    rows, columns = codes.shape
    block = rows // 2
    groups = block // GROUP

    def kernel(codes_ref, steps_ref, out):
        for k in range(groups):
            group = slice(k * GROUP, (k + 1) * GROUP)
            centered = (codes_ref[group, :] - 8).astype(F32)
            step = steps_ref[pl.ds(pl.program_id(0) * groups + k, 1), :]
            out[:, group] = (centered * step).astype(BF16).T

    return pl.pallas_call(
        kernel,
        out_shape=jax.ShapeDtypeStruct((columns, rows), BF16),
        grid=(rows // block,),
        in_specs=[
            pl.BlockSpec((block, columns), lambda k: (k, 0)),
            pl.BlockSpec(steps.shape, lambda k: (0, 0)),
        ],
        out_specs=pl.BlockSpec((columns, block), lambda k: (0, k)),
        cost_estimate=BRIEF,
    )(codes, steps)


def attention_probs(queries, keys, segment_ids, first, count):
    length = keys.shape[0]

    def kernel(q_ref, k_ref, down_ref, along_ref, out, allowed):
        @pl.when(pl.program_id(0) == 0)
        def _():
            key_at = lax.broadcasted_iota(jnp.int32, (length, length), 0)
            query_at = lax.broadcasted_iota(jnp.int32, (length, length), 1)
            seen = (key_at <= query_at) & (down_ref[...] == along_ref[...])
            allowed[...] = seen.astype(F32)

        scores = lax.dot_general(
            k_ref[...], q_ref[...], (((1,), (1,)), ((), ())), preferred_element_type=F32
        ) * HD ** (-0.5)
        scores = jnp.where(allowed[...] > 0.5, scores, -1e30)
        powers = jnp.exp(scores - jnp.max(scores, axis=0, keepdims=True))
        out[0] = (powers / jnp.sum(powers, axis=0, keepdims=True)).astype(BF16)

    return pl.pallas_call(
        kernel,
        out_shape=jax.ShapeDtypeStruct((count, length, length), BF16),
        grid=(count,),
        in_specs=[
            pl.BlockSpec((length, HD), lambda h: (0, first + h)),
            pl.BlockSpec((length, HD), lambda h: (0, 0)),
            pl.BlockSpec((length, 1), lambda h: (0, 0)),
            pl.BlockSpec((1, length), lambda h: (0, 0)),
        ],
        out_specs=pl.BlockSpec((1, length, length), lambda h: (h, 0, 0)),
        scratch_shapes=[pltpu.VMEM((length, length), F32)],
        compiler_params=pltpu.CompilerParams(vmem_limit_bytes=32 << 20),
        cost_estimate=LONG,
    )(queries, keys, segment_ids.reshape(length, 1), segment_ids)


def attended_heads(hidden_in, value_weight, probs):
    width, columns = value_weight.shape
    rows = hidden_in.shape[0]
    heads = 2 * probs[0].shape[0]
    count = 8
    depth = width // count

    def kernel(h_ref, v_ref, p_low, p_high, out, total):
        k = pl.program_id(0)
        more = jnp.dot(h_ref[...], v_ref[...], preferred_element_type=F32)

        @pl.when(k == 0)
        def _():
            total[...] = more

        @pl.when(k > 0)
        def _():
            total[...] += more

        @pl.when(k == count - 1)
        def _():
            values = total[...].T.astype(BF16)
            for h in range(heads):
                p_ref = (p_low, p_high)[h // (heads // 2)]
                one = jnp.dot(values, p_ref[h % (heads // 2)], preferred_element_type=F32)
                out[h * columns : (h + 1) * columns, :] = one.astype(BF16)

    whole = pl.BlockSpec(probs[0].shape, lambda k: (0, 0, 0))
    return pl.pallas_call(
        kernel,
        out_shape=jax.ShapeDtypeStruct((heads * columns, rows), BF16),
        grid=(count,),
        in_specs=[
            pl.BlockSpec((rows, depth), lambda k: (0, k)),
            pl.BlockSpec((depth, columns), lambda k: (k, 0)),
            whole,
            whole,
        ],
        out_specs=pl.BlockSpec((heads * columns, rows), lambda k: (0, 0)),
        scratch_shapes=[pltpu.VMEM((rows, columns), F32)],
        compiler_params=pltpu.CompilerParams(vmem_limit_bytes=56 << 20),
        cost_estimate=LONG,
    )(hidden_in, value_weight, *probs)


def value_terms(hidden_in, here, there, probs, own_order, other_order):
    (count,) = own_order.shape
    rows = here.shape[0]
    width = hidden_in.shape[1] // (2 * count)
    half = probs[0].shape[0]

    def kernel(own_at, other_at, h_ref, a_ref, b_ref, p_low, p_high, *refs):
        own_out, other_out, held, total, grad, sem = refs
        fetch = pltpu.make_async_copy(h_ref, held, sem)
        fetch.start()
        for h in range(2 * half):
            head = slice(h * HD, (h + 1) * HD)
            attended_grad = (a_ref[:, head] + b_ref[:, head].astype(F32)).astype(BF16)
            more = jnp.dot(
                (p_low, p_high)[h // half][h % half], attended_grad, preferred_element_type=F32
            )
            if h == 0:
                total[...] = more
            else:
                total[...] += more
        grad[...] = total[...].T.astype(BF16)
        fetch.wait()

        def one(k, carry):
            def product(at):
                block = held[:, pl.ds(pl.multiple_of(at * width, width), width)]
                return jnp.dot(grad[...], block, preferred_element_type=F32)

            own_out[k] = product(own_at[k])
            other_out[k] = product(other_at[k]).astype(BF16)
            return carry

        lax.fori_loop(0, count, one, 0)

    whole = pl.BlockSpec(memory_space=pltpu.VMEM)
    return pl.pallas_call(
        kernel,
        out_shape=(
            jax.ShapeDtypeStruct((count, HD, width), F32),
            jax.ShapeDtypeStruct((count, HD, width), BF16),
        ),
        grid_spec=pltpu.PrefetchScalarGridSpec(
            num_scalar_prefetch=2,
            in_specs=[pl.BlockSpec(memory_space=pl.ANY)] + [whole] * 4,
            out_specs=(whole, whole),
            scratch_shapes=[
                pltpu.VMEM(hidden_in.shape, BF16),
                pltpu.VMEM((rows, HD), F32),
                pltpu.VMEM((HD, rows), BF16),
                pltpu.SemaphoreType.DMA,
            ],
        ),
        compiler_params=pltpu.CompilerParams(vmem_limit_bytes=56 << 20),
        cost_estimate=BRIEF,
    )(own_order, other_order, hidden_in, here, there, *probs)


def value_grads(own, others, codes):
    columns, rows = own.shape

    def kernel(own_ref, *refs):
        refs, (codes_ref, step_out, out) = refs[: len(others)], refs[len(others) :]
        total = own_ref[...]
        for ref in refs:
            total += ref[...].astype(F32)
        total = total.T
        out[...] = total
        centered = (codes_ref[...] - 8).astype(F32) * total
        for k in range(rows // GROUP):
            group = centered[k * GROUP : (k + 1) * GROUP]
            step_out[k : k + 1, :] = jnp.sum(group, axis=0, keepdims=True)

    return pl.pallas_call(
        kernel,
        out_shape=(
            jax.ShapeDtypeStruct((rows // GROUP, columns), F32),
            jax.ShapeDtypeStruct((rows, columns), F32),
        ),
        cost_estimate=BRIEF,
    )(own, *others, codes)


def fetch_piece(which, pieces, target, sem):
    for i, piece in enumerate(pieces):

        @pl.when(which == i)
        def _():
            pltpu.make_async_copy(piece, target, sem).start()


def head_grads(grads, weights, which, use, so_far=None):
    count, numbers = len(weights), list(grads)
    (rows, depth), heads = grads[numbers[0]].shape, weights[0].shape[1]
    half = rows // 2
    last = so_far is not None

    def kernel(which_ref, use_ref, *refs):
        g_refs, refs = refs[: len(grads)], refs[len(grads) :]
        w_refs, refs = refs[:count], refs[count:]
        g_held, w_held, g_sems, w_sems = refs[-4:]
        if last:
            before, own, other, total, sem = refs[:-4]
            start = pltpu.make_async_copy(before, total, sem)
            start.start()
        else:
            (total,) = refs[:-4]
        for k in range(count):

            @pl.when(use_ref[k] == 1)
            def _():
                for number, g_ref in zip(numbers, g_refs):

                    @pl.when(which_ref[k] == number)
                    def _():
                        pltpu.make_async_copy(g_ref, g_held.at[k], g_sems.at[k]).start()

                pltpu.make_async_copy(w_refs[k], w_held.at[k], w_sems.at[k]).start()

        if last:
            start.wait()
        else:
            total[...] = jnp.zeros_like(total)

        def one(k, carry):
            @pl.when(use_ref[k] == 1)
            def _():
                pltpu.make_async_copy(g_refs[0], g_held.at[k], g_sems.at[k]).wait()
                pltpu.make_async_copy(w_refs[0], w_held.at[k], w_sems.at[k]).wait()
                total[...] += jnp.dot(g_held[k], w_held[k], preferred_element_type=F32)

            return carry

        lax.fori_loop(0, count, one, 0)
        if last:
            own[...] = total[:half]
            other[...] = total[half:].astype(BF16)

    whole = pl.BlockSpec(memory_space=pltpu.VMEM)
    anywhere = pl.BlockSpec(memory_space=pl.ANY)
    scratch = [
        pltpu.VMEM((count, rows, depth), BF16),
        pltpu.VMEM((count, depth, heads), BF16),
        pltpu.SemaphoreType.DMA((count,)),
        pltpu.SemaphoreType.DMA((count,)),
    ]
    if last:
        scratch = [pltpu.VMEM((rows, heads), F32), pltpu.SemaphoreType.DMA] + scratch
        out_shape = (
            jax.ShapeDtypeStruct((half, heads), F32),
            jax.ShapeDtypeStruct((half, heads), BF16),
        )
    else:
        out_shape = jax.ShapeDtypeStruct((rows, heads), F32)
    return pl.pallas_call(
        kernel,
        out_shape=out_shape,
        grid_spec=pltpu.PrefetchScalarGridSpec(
            num_scalar_prefetch=2,
            in_specs=[anywhere] * (len(grads) + count + last),
            out_specs=(whole, whole) if last else whole,
            scratch_shapes=scratch,
        ),
        compiler_params=pltpu.CompilerParams(vmem_limit_bytes=52 << 20),
        cost_estimate=BRIEF,
    )(which, use, *grads.values(), *weights, *([so_far] if last else []))


def weight_parts(attended, grads, order):
    (count,) = order.shape
    rows, depth = grads[0].shape
    heads, half = attended[0].shape
    tile = 256

    def kernel(order_ref, first, second, *refs):
        g_refs, outs, refs = refs[: len(grads)], refs[len(grads) : -6], refs[-6:]
        a_held, held, done, a_sem, sems, out_sems = refs
        a_copies = [
            pltpu.make_async_copy(first, a_held.at[:, :half], a_sem.at[0]),
            pltpu.make_async_copy(second, a_held.at[:, half:], a_sem.at[1]),
        ]
        for copy in a_copies:
            copy.start()
        for k in range(count):
            fetch_piece(order_ref[k], g_refs, held.at[k], sems.at[k])
        for copy in a_copies:
            copy.wait()
        out_copies = []
        for k in range(count):
            pltpu.make_async_copy(g_refs[0], held.at[k], sems.at[k]).wait()
            for n in range(0, depth, tile):
                block = held[k, :, n : n + tile]
                one = jnp.dot(a_held[...], block, preferred_element_type=F32)
                done[k, :, n : n + tile] = one.astype(BF16)
            out_copies.append(pltpu.make_async_copy(done.at[k], outs[k], out_sems.at[k]))
            out_copies[-1].start()
        for copy in out_copies:
            copy.wait()

    anywhere = pl.BlockSpec(memory_space=pl.ANY)
    return pl.pallas_call(
        kernel,
        out_shape=(jax.ShapeDtypeStruct((heads, depth), BF16),) * count,
        grid_spec=pltpu.PrefetchScalarGridSpec(
            num_scalar_prefetch=1,
            in_specs=[anywhere] * (2 + len(grads)),
            out_specs=(anywhere,) * count,
            scratch_shapes=[
                pltpu.VMEM((heads, rows), BF16),
                pltpu.VMEM((count, rows, depth), BF16),
                pltpu.VMEM((count, heads, depth), BF16),
                pltpu.SemaphoreType.DMA((2,)),
                pltpu.SemaphoreType.DMA((count,)),
                pltpu.SemaphoreType.DMA((count,)),
            ],
        ),
        compiler_params=pltpu.CompilerParams(vmem_limit_bytes=48 << 20),
        cost_estimate=BRIEF,
    )(order, *attended, *grads)


def gate(arrays, *after):
    flat, tree = jax.tree.flatten((arrays, after))
    return jax.tree.unflatten(tree, lax.optimization_barrier(flat))[0]


def body(
    hidden_in,
    out_grad,
    queries,
    keys,
    segment_ids,
    value_codes,
    value_steps,
    output_codes,
    output_steps,
):
    xh, y, c, z, xl = (lax.axis_index(a) for a in SIZES)
    heads, half = output_codes.shape

    others = [(distance, side) for distance in range(4) for side in (0, 1)]

    def chip_at(distance, side):
        return (xh ^ side) * 4 + (y + distance) % 4

    chips = jnp.stack([chip_at(*key) for key in others]).astype(jnp.int32)
    own_order, other_order = chips * 2 + c, chips * 2 + 1 - c

    def piece_at(distance, side):
        chip = chip_at(distance, side)
        return ((chip // 2 - z) % 4) * 2 + ((chip % 2) ^ xl)

    def pieces_at(keys_of):
        return jnp.stack([piece_at(*key) for key in keys_of]).astype(jnp.int32)

    value_weight = lax.all_gather(dequant_rows(value_codes, value_steps), ROWS, axis=0, tiled=True)
    keep = lax.dynamic_slice_in_dim(out_grad, c * half, half, 1)
    give = lax.dynamic_slice_in_dim(out_grad, (1 - c) * half, half, 1)
    grads = jnp.concatenate([keep, shift(give, "c", 1)], axis=0)
    weight = dequant_transposed(output_codes, output_steps)
    grads, weight, queries = gate((grads, weight, queries))

    g, w = {(0, 0): grads}, {(0, 0): weight}
    w[3, 0], w[1, 0] = shift(weight, "y", 1), shift(weight, "y", -1)
    g[3, 0], g[1, 0] = shift(grads, "z", 1), shift(grads, "z", -1)
    g[0, 1] = shift(grads, "xl", 1)
    probs = [attention_probs(queries, keys, segment_ids, h, GQ // 2) for h in (0, GQ // 2)]
    g, w, probs = gate((g, w, probs))

    g[3, 1], g[1, 1] = shift(g[0, 1], "z", 1), shift(g[0, 1], "z", -1)
    w[0, 1] = shift(weight, "xh", 1)
    w[2, 0] = shift(w[3, 0], "y", 1)
    g, w, value_weight, probs = gate((g, w, value_weight, probs))

    w[3, 1], w[1, 1] = shift(w[0, 1], "y", 1), shift(w[0, 1], "y", -1)
    w[2, 1] = shift(w[2, 0], "xh", 1)
    g[2, 0], g[2, 1] = shift(g[3, 0], "z", 1), shift(g[1, 1], "z", -1)
    attended = attended_heads(hidden_in, value_weight, probs)

    early = [(0, 0), (1, 0), (2, 0), (3, 0), (0, 1)]
    at_hand = {2 * d + s: g[d, s] for d, s in others if d != 2}
    at_hand, early_weights, attended = gate((at_hand, [w[key] for key in early], attended))
    use = (pieces_at(early) // 2 != 2).astype(jnp.int32)
    so_far = head_grads(at_hand, early_weights, pieces_at(early), use)
    g, w, attended, probs, so_far = gate((g, w, attended, probs, so_far))

    attended = attended, shift(attended, "c", 1)
    pieces = [g[key] for key in others]
    use = jnp.stack([jnp.where(key in early, piece_at(*key) // 2 == 2, True) for key in others])
    here, there = head_grads(
        dict(enumerate(pieces)),
        [w[key] for key in others],
        pieces_at(others),
        use.astype(jnp.int32),
        so_far,
    )
    here, there, pieces, attended = gate((here, there, pieces, attended))
    there = shift(there, "c", 1)
    up1, down1, cross = weight_parts(attended, pieces, pieces_at([(1, 1), (3, 1), (2, 1)]))
    here, there, up1, down1, cross = gate((here, there, up1, down1, cross))
    up1, down1, cross = shift(up1, "y", 1), shift(down1, "y", -1), shift(cross, "xh", 1)
    term, term_give = value_terms(hidden_in, here, there, probs, own_order, other_order)
    term, term_give, attended, pieces = gate((term, term_give, attended, pieces))
    far_part, across, up_part, down_part, stay = weight_parts(
        attended, pieces, pieces_at([(2, 0), (0, 1), (1, 0), (3, 0), (0, 0)])
    )
    term, term_give, up1, down1, cross, far_part, across, up_part, down_part, stay = gate(
        (term, term_give, up1, down1, cross, far_part, across, up_part, down_part, stay)
    )

    term = (term + shift(term_give, "c", 1).astype(F32)).reshape(4, 2, HD, half)
    term, term_give = term[:, 0], shift(term[:, 1].astype(BF16), "xh", 1)
    far_part = (far_part.astype(F32) + cross.astype(F32)).astype(BF16)
    low = shift(far_part[: heads // 2], "y", 1)
    high = shift(far_part[heads // 2 :], "y", -1)
    across = (across.astype(F32) + up1.astype(F32) + down1.astype(F32)).astype(BF16)
    low, high, across, up_part, down_part, stay, term, term_give = gate(
        (low, high, across, up_part, down_part, stay, term, term_give)
    )

    across = shift(across, "xh", 1)
    term = term + term_give.astype(F32)
    send = term.astype(BF16)
    low, high = low.astype(F32), high.astype(F32)
    up0, down0 = up_part.astype(F32), down_part.astype(F32)
    up0 = jnp.concatenate(
        [(up0[: heads // 2] + low).astype(BF16), up_part[heads // 2 :], send[1]], axis=0
    )
    down0 = jnp.concatenate(
        [down_part[: heads // 2], (down0[heads // 2 :] + high).astype(BF16), send[3]], axis=0
    )
    up0, down0 = shift(up0, "y", 1), shift(down0, "y", -1)
    term_far = shift(send[2], "y", 2)
    terms = (up0[heads:], down0[heads:], term_far)
    value_step_grad, value_weight_grad = value_grads(term[0], terms, value_codes)
    output_weight_grad = stay.astype(F32) + across.astype(F32)
    output_weight_grad += up0[:heads].astype(F32) + down0[:heads].astype(F32)
    centered_out = (output_codes - 8).astype(F32)
    output_step_grad = (centered_out * output_weight_grad).reshape(-1, GROUP, half).sum(axis=1)
    return (output_step_grad, value_step_grad, output_weight_grad, value_weight_grad)


def solution(mesh):
    fine = Mesh(mesh.devices.reshape(tuple(SIZES.values())), tuple(SIZES))
    return jax.shard_map(
        body,
        mesh=fine,
        in_specs=(
            P(ROWS, None),
            P(ROWS, HEADS_AXES),
            P(ROWS, HEADS_AXES),
            P(ROWS, HEADS_AXES),
            P(ROWS, None),
            P(ROWS, HEADS_AXES),
            P(ROWS, HEADS_AXES),
            P(HEADS_AXES, ROWS),
            P(HEADS_AXES, ROWS),
        ),
        out_specs=(
            P(HEADS_AXES, ROWS),
            P(ROWS, HEADS_AXES),
            P(HEADS_AXES, ROWS),
            P(ROWS, HEADS_AXES),
        ),
        check_vma=False,
    )
```

```python
import jax
import jax.numpy as jnp
from jax import lax
from jax.experimental import pallas as pl
from jax.experimental.pallas import tpu as pltpu
from jax.sharding import Mesh, PartitionSpec as P

HD = 128
GROUP = 128
GQ = 8
SIZES = {"xh": 2, "y": 4, "c": 2, "z": 4, "xl": 2}
ROWS = ("xh", "y", "c")
HEADS_AXES = ("z", "xl")
F32 = jnp.float32
BF16 = jnp.bfloat16
LONG = pl.CostEstimate(flops=1 << 35, bytes_accessed=1 << 24, transcendentals=0)
BRIEF = pl.CostEstimate(flops=1 << 20, bytes_accessed=1 << 16, transcendentals=0)


def shift(x, axis, step):
    n = SIZES[axis]
    return lax.ppermute(x, axis, [(i, (i + step) % n) for i in range(n)])


def dequant_rows(codes, steps):
    rows, columns = codes.shape

    def kernel(codes_ref, steps_ref, out):
        for k in range(rows // GROUP):
            group = slice(k * GROUP, (k + 1) * GROUP)
            centered = (codes_ref[group, :] - 8).astype(F32)
            out[group, :] = (centered * steps_ref[k : k + 1, :]).astype(BF16)

    return pl.pallas_call(
        kernel,
        out_shape=jax.ShapeDtypeStruct((rows, columns), BF16),
        cost_estimate=BRIEF,
    )(codes, steps)


def dequant_transposed(codes, steps):
    rows, columns = codes.shape
    block = rows // 2
    groups = block // GROUP

    def kernel(codes_ref, steps_ref, out):
        for k in range(groups):
            group = slice(k * GROUP, (k + 1) * GROUP)
            centered = (codes_ref[group, :] - 8).astype(F32)
            step = steps_ref[pl.ds(pl.program_id(0) * groups + k, 1), :]
            out[:, group] = (centered * step).astype(BF16).T

    return pl.pallas_call(
        kernel,
        out_shape=jax.ShapeDtypeStruct((columns, rows), BF16),
        grid=(rows // block,),
        in_specs=[
            pl.BlockSpec((block, columns), lambda k: (k, 0)),
            pl.BlockSpec(steps.shape, lambda k: (0, 0)),
        ],
        out_specs=pl.BlockSpec((columns, block), lambda k: (0, k)),
        cost_estimate=BRIEF,
    )(codes, steps)


def attention_probs(queries, keys, segment_ids, first, count):
    length = keys.shape[0]

    def kernel(q_ref, k_ref, down_ref, along_ref, out, allowed):
        @pl.when(pl.program_id(0) == 0)
        def _():
            key_at = lax.broadcasted_iota(jnp.int32, (length, length), 0)
            query_at = lax.broadcasted_iota(jnp.int32, (length, length), 1)
            seen = (key_at <= query_at) & (down_ref[...] == along_ref[...])
            allowed[...] = seen.astype(F32)

        scores = lax.dot_general(
            k_ref[...], q_ref[...], (((1,), (1,)), ((), ())), preferred_element_type=F32
        ) * HD ** (-0.5)
        scores = jnp.where(allowed[...] > 0.5, scores, -1e30)
        powers = jnp.exp(scores - jnp.max(scores, axis=0, keepdims=True))
        out[0] = (powers / jnp.sum(powers, axis=0, keepdims=True)).astype(BF16)

    return pl.pallas_call(
        kernel,
        out_shape=jax.ShapeDtypeStruct((count, length, length), BF16),
        grid=(count,),
        in_specs=[
            pl.BlockSpec((length, HD), lambda h: (0, first + h)),
            pl.BlockSpec((length, HD), lambda h: (0, 0)),
            pl.BlockSpec((length, 1), lambda h: (0, 0)),
            pl.BlockSpec((1, length), lambda h: (0, 0)),
        ],
        out_specs=pl.BlockSpec((1, length, length), lambda h: (h, 0, 0)),
        scratch_shapes=[pltpu.VMEM((length, length), F32)],
        compiler_params=pltpu.CompilerParams(vmem_limit_bytes=32 << 20),
        cost_estimate=LONG,
    )(queries, keys, segment_ids.reshape(length, 1), segment_ids)


def attended_heads(hidden_in, value_weight, probs):
    width, columns = value_weight.shape
    rows = hidden_in.shape[0]
    heads = 2 * probs[0].shape[0]
    count = 8
    depth = width // count

    def kernel(h_ref, v_ref, p_low, p_high, out, total):
        k = pl.program_id(0)
        more = jnp.dot(h_ref[...], v_ref[...], preferred_element_type=F32)

        @pl.when(k == 0)
        def _():
            total[...] = more

        @pl.when(k > 0)
        def _():
            total[...] += more

        @pl.when(k == count - 1)
        def _():
            values = total[...].T.astype(BF16)
            for h in range(heads):
                p_ref = (p_low, p_high)[h // (heads // 2)]
                one = jnp.dot(values, p_ref[h % (heads // 2)], preferred_element_type=F32)
                out[h * columns : (h + 1) * columns, :] = one.astype(BF16)

    whole = pl.BlockSpec(probs[0].shape, lambda k: (0, 0, 0))
    return pl.pallas_call(
        kernel,
        out_shape=jax.ShapeDtypeStruct((heads * columns, rows), BF16),
        grid=(count,),
        in_specs=[
            pl.BlockSpec((rows, depth), lambda k: (0, k)),
            pl.BlockSpec((depth, columns), lambda k: (k, 0)),
            whole,
            whole,
        ],
        out_specs=pl.BlockSpec((heads * columns, rows), lambda k: (0, 0)),
        scratch_shapes=[pltpu.VMEM((rows, columns), F32)],
        compiler_params=pltpu.CompilerParams(vmem_limit_bytes=56 << 20),
        cost_estimate=LONG,
    )(hidden_in, value_weight, *probs)


def value_terms(hidden_in, here, there, probs, own_order, other_order):
    (count,) = own_order.shape
    rows = here.shape[0]
    width = hidden_in.shape[1] // (2 * count)
    half = probs[0].shape[0]

    def kernel(own_at, other_at, h_ref, a_ref, b_ref, p_low, p_high, *refs):
        own_out, other_out, held, total, grad, sem = refs
        fetch = pltpu.make_async_copy(h_ref, held, sem)
        fetch.start()
        for h in range(2 * half):
            head = slice(h * HD, (h + 1) * HD)
            attended_grad = (a_ref[:, head] + b_ref[:, head].astype(F32)).astype(BF16)
            more = jnp.dot(
                (p_low, p_high)[h // half][h % half], attended_grad, preferred_element_type=F32
            )
            if h == 0:
                total[...] = more
            else:
                total[...] += more
        grad[...] = total[...].T.astype(BF16)
        fetch.wait()

        def one(k, carry):
            def product(at):
                block = held[:, pl.ds(pl.multiple_of(at * width, width), width)]
                return jnp.dot(grad[...], block, preferred_element_type=F32)

            own_out[k] = product(own_at[k])
            other_out[k] = product(other_at[k]).astype(BF16)
            return carry

        lax.fori_loop(0, count, one, 0)

    whole = pl.BlockSpec(memory_space=pltpu.VMEM)
    return pl.pallas_call(
        kernel,
        out_shape=(
            jax.ShapeDtypeStruct((count, HD, width), F32),
            jax.ShapeDtypeStruct((count, HD, width), BF16),
        ),
        grid_spec=pltpu.PrefetchScalarGridSpec(
            num_scalar_prefetch=2,
            in_specs=[pl.BlockSpec(memory_space=pl.ANY)] + [whole] * 4,
            out_specs=(whole, whole),
            scratch_shapes=[
                pltpu.VMEM(hidden_in.shape, BF16),
                pltpu.VMEM((rows, HD), F32),
                pltpu.VMEM((HD, rows), BF16),
                pltpu.SemaphoreType.DMA,
            ],
        ),
        compiler_params=pltpu.CompilerParams(vmem_limit_bytes=56 << 20),
        cost_estimate=BRIEF,
    )(own_order, other_order, hidden_in, here, there, *probs)


def final_grads(weight_terms, value_terms, output_codes, value_codes):
    rows, columns = output_codes.shape
    depth, width = value_codes.shape
    steps = 4
    block = rows // steps
    groups = block // GROUP
    count = len(weight_terms)

    def centered_sums(codes, total, step_out, first):
        centered = (codes - 8).astype(F32) * total
        for k in range(total.shape[0] // GROUP):
            group = centered[k * GROUP : (k + 1) * GROUP]
            step_out[pl.ds(first + k, 1), :] = jnp.sum(group, axis=0, keepdims=True)

    def kernel(*refs):
        terms, refs = refs[:count], refs[count:]
        value_refs, refs = refs[: 2 + len(value_terms)], refs[2 + len(value_terms) :]
        codes_ref, value_codes_ref, step_out, value_step_out, out, value_out = refs
        k = pl.program_id(0)
        total = terms[0][...].astype(F32)
        for ref in terms[1:]:
            total += ref[...].astype(F32)
        out[...] = total
        centered_sums(codes_ref[...], total, step_out, k * groups)

        @pl.when(k == 0)
        def _():
            value = value_refs[0][...].astype(F32)
            for ref in value_refs[1:]:
                value += ref[...].astype(F32)
            value = value.T
            value_out[...] = value
            centered_sums(value_codes_ref[...], value, value_step_out, 0)

    part = pl.BlockSpec((block, columns), lambda k: (k, 0))
    below = pl.BlockSpec((width, columns), lambda k: (rows // width, 0))

    def whole(shape):
        return pl.BlockSpec(shape, lambda k: (0,) * len(shape))

    step_shape, value_step_shape = (rows // GROUP, columns), (depth // GROUP, width)
    return pl.pallas_call(
        kernel,
        out_shape=tuple(
            jax.ShapeDtypeStruct(shape, F32)
            for shape in (step_shape, value_step_shape, output_codes.shape, value_codes.shape)
        ),
        grid=(steps,),
        in_specs=[part] * count
        + [below] * 2
        + [whole(x.shape) for x in value_terms]
        + [part, whole(value_codes.shape)],
        out_specs=(whole(step_shape), whole(value_step_shape), part, whole(value_codes.shape)),
        compiler_params=pltpu.CompilerParams(vmem_limit_bytes=32 << 20),
        cost_estimate=BRIEF,
    )(*weight_terms, *weight_terms[-2:], *value_terms, output_codes, value_codes)


def fetch_piece(which, pieces, target, sem):
    for i, piece in enumerate(pieces):

        @pl.when(which == i)
        def _():
            pltpu.make_async_copy(piece, target, sem).start()


def head_grads(grads, weights, which, use, so_far=None):
    count, numbers = len(weights), list(grads)
    (rows, depth), heads = grads[numbers[0]].shape, weights[0].shape[1]
    half = rows // 2
    last = so_far is not None

    def kernel(which_ref, use_ref, *refs):
        g_refs, refs = refs[: len(grads)], refs[len(grads) :]
        w_refs, refs = refs[:count], refs[count:]
        g_held, w_held, g_sems, w_sems = refs[-4:]
        if last:
            before, own, other, total, sem = refs[:-4]
            start = pltpu.make_async_copy(before, total, sem)
            start.start()
        else:
            (total,) = refs[:-4]
        for k in range(count):

            @pl.when(use_ref[k] == 1)
            def _():
                for number, g_ref in zip(numbers, g_refs):

                    @pl.when(which_ref[k] == number)
                    def _():
                        pltpu.make_async_copy(g_ref, g_held.at[k], g_sems.at[k]).start()

                pltpu.make_async_copy(w_refs[k], w_held.at[k], w_sems.at[k]).start()

        if last:
            start.wait()
        else:
            total[...] = jnp.zeros_like(total)

        def one(k, carry):
            @pl.when(use_ref[k] == 1)
            def _():
                pltpu.make_async_copy(g_refs[0], g_held.at[k], g_sems.at[k]).wait()
                pltpu.make_async_copy(w_refs[0], w_held.at[k], w_sems.at[k]).wait()
                total[...] += jnp.dot(g_held[k], w_held[k], preferred_element_type=F32)

            return carry

        lax.fori_loop(0, count, one, 0)
        if last:
            own[...] = total[:half]
            other[...] = total[half:].astype(BF16)

    whole = pl.BlockSpec(memory_space=pltpu.VMEM)
    anywhere = pl.BlockSpec(memory_space=pl.ANY)
    scratch = [
        pltpu.VMEM((count, rows, depth), BF16),
        pltpu.VMEM((count, depth, heads), BF16),
        pltpu.SemaphoreType.DMA((count,)),
        pltpu.SemaphoreType.DMA((count,)),
    ]
    if last:
        scratch = [pltpu.VMEM((rows, heads), F32), pltpu.SemaphoreType.DMA] + scratch
        out_shape = (
            jax.ShapeDtypeStruct((half, heads), F32),
            jax.ShapeDtypeStruct((half, heads), BF16),
        )
    else:
        out_shape = jax.ShapeDtypeStruct((rows, heads), F32)
    return pl.pallas_call(
        kernel,
        out_shape=out_shape,
        grid_spec=pltpu.PrefetchScalarGridSpec(
            num_scalar_prefetch=2,
            in_specs=[anywhere] * (len(grads) + count + last),
            out_specs=(whole, whole) if last else whole,
            scratch_shapes=scratch,
        ),
        compiler_params=pltpu.CompilerParams(vmem_limit_bytes=52 << 20),
        cost_estimate=BRIEF,
    )(which, use, *grads.values(), *weights, *([so_far] if last else []))


def weight_parts(attended, grads, order):
    (count,) = order.shape
    rows, depth = grads[0].shape
    heads, half = attended[0].shape
    tile = 256

    def kernel(order_ref, first, second, *refs):
        g_refs, outs, refs = refs[: len(grads)], refs[len(grads) : -6], refs[-6:]
        a_held, held, done, a_sem, sems, out_sems = refs
        a_copies = [
            pltpu.make_async_copy(first, a_held.at[:, :half], a_sem.at[0]),
            pltpu.make_async_copy(second, a_held.at[:, half:], a_sem.at[1]),
        ]
        for copy in a_copies:
            copy.start()
        for k in range(count):
            fetch_piece(order_ref[k], g_refs, held.at[k], sems.at[k])
        for copy in a_copies:
            copy.wait()
        out_copies = []
        for k in range(count):
            pltpu.make_async_copy(g_refs[0], held.at[k], sems.at[k]).wait()
            for n in range(0, depth, tile):
                block = held[k, :, n : n + tile]
                one = jnp.dot(a_held[...], block, preferred_element_type=F32)
                done[k, :, n : n + tile] = one.astype(BF16)
            out_copies.append(pltpu.make_async_copy(done.at[k], outs[k], out_sems.at[k]))
            out_copies[-1].start()
        for copy in out_copies:
            copy.wait()

    anywhere = pl.BlockSpec(memory_space=pl.ANY)
    return pl.pallas_call(
        kernel,
        out_shape=(jax.ShapeDtypeStruct((heads, depth), BF16),) * count,
        grid_spec=pltpu.PrefetchScalarGridSpec(
            num_scalar_prefetch=1,
            in_specs=[anywhere] * (2 + len(grads)),
            out_specs=(anywhere,) * count,
            scratch_shapes=[
                pltpu.VMEM((heads, rows), BF16),
                pltpu.VMEM((count, rows, depth), BF16),
                pltpu.VMEM((count, heads, depth), BF16),
                pltpu.SemaphoreType.DMA((2,)),
                pltpu.SemaphoreType.DMA((count,)),
                pltpu.SemaphoreType.DMA((count,)),
            ],
        ),
        compiler_params=pltpu.CompilerParams(vmem_limit_bytes=48 << 20),
        cost_estimate=BRIEF,
    )(order, *attended, *grads)


def gate(arrays, *after):
    flat, tree = jax.tree.flatten((arrays, after))
    return jax.tree.unflatten(tree, lax.optimization_barrier(flat))[0]


def body(
    hidden_in,
    out_grad,
    queries,
    keys,
    segment_ids,
    value_codes,
    value_steps,
    output_codes,
    output_steps,
):
    xh, y, c, z, xl = (lax.axis_index(a) for a in SIZES)
    heads, half = output_codes.shape

    others = [(distance, side) for distance in range(4) for side in (0, 1)]

    def chip_at(distance, side):
        return (xh ^ side) * 4 + (y + distance) % 4

    chips = jnp.stack([chip_at(*key) for key in others]).astype(jnp.int32)
    own_order, other_order = chips * 2 + c, chips * 2 + 1 - c

    def piece_at(distance, side):
        chip = chip_at(distance, side)
        return ((chip // 2 - z) % 4) * 2 + ((chip % 2) ^ xl)

    def pieces_at(keys_of):
        return jnp.stack([piece_at(*key) for key in keys_of]).astype(jnp.int32)

    value_weight = lax.all_gather(dequant_rows(value_codes, value_steps), ROWS, axis=0, tiled=True)
    keep = lax.dynamic_slice_in_dim(out_grad, c * half, half, 1)
    give = lax.dynamic_slice_in_dim(out_grad, (1 - c) * half, half, 1)
    grads = jnp.concatenate([keep, shift(give, "c", 1)], axis=0)
    weight = dequant_transposed(output_codes, output_steps)
    grads, weight, queries = gate((grads, weight, queries))

    g, w = {(0, 0): grads}, {(0, 0): weight}
    w[3, 0], w[1, 0] = shift(weight, "y", 1), shift(weight, "y", -1)
    g[3, 0], g[1, 0] = shift(grads, "z", 1), shift(grads, "z", -1)
    g[0, 1] = shift(grads, "xl", 1)
    probs = [attention_probs(queries, keys, segment_ids, h, GQ // 2) for h in (0, GQ // 2)]
    g, w, probs = gate((g, w, probs))

    g[3, 1], g[1, 1] = shift(g[0, 1], "z", 1), shift(g[0, 1], "z", -1)
    w[0, 1] = shift(weight, "xh", 1)
    w[2, 0] = shift(w[3, 0], "y", 1)
    g, w, value_weight, probs = gate((g, w, value_weight, probs))

    w[3, 1], w[1, 1] = shift(w[0, 1], "y", 1), shift(w[0, 1], "y", -1)
    w[2, 1] = shift(w[2, 0], "xh", 1)
    g[2, 0], g[2, 1] = shift(g[3, 0], "z", 1), shift(g[1, 1], "z", -1)
    attended = attended_heads(hidden_in, value_weight, probs)

    early = [(0, 0), (1, 0), (2, 0), (3, 0), (0, 1)]
    at_hand = {2 * d + s: g[d, s] for d, s in others if d != 2}
    at_hand, early_weights, attended = gate((at_hand, [w[key] for key in early], attended))
    use = (pieces_at(early) // 2 != 2).astype(jnp.int32)
    so_far = head_grads(at_hand, early_weights, pieces_at(early), use)
    g, w, attended, probs, so_far = gate((g, w, attended, probs, so_far))

    attended = attended, shift(attended, "c", 1)
    pieces = [g[key] for key in others]
    use = jnp.stack([jnp.where(key in early, piece_at(*key) // 2 == 2, True) for key in others])
    here, there = head_grads(
        dict(enumerate(pieces)),
        [w[key] for key in others],
        pieces_at(others),
        use.astype(jnp.int32),
        so_far,
    )
    here, there, pieces, attended = gate((here, there, pieces, attended))
    there = shift(there, "c", 1)
    up1, down1, cross = weight_parts(attended, pieces, pieces_at([(1, 1), (3, 1), (2, 1)]))
    here, there, up1, down1, cross = gate((here, there, up1, down1, cross))
    up1, down1, cross = shift(up1, "y", 1), shift(down1, "y", -1), shift(cross, "xh", 1)
    term, term_give = value_terms(hidden_in, here, there, probs, own_order, other_order)
    term, term_give, attended, pieces = gate((term, term_give, attended, pieces))
    far_part, across, up_part, down_part, stay = weight_parts(
        attended, pieces, pieces_at([(2, 0), (0, 1), (1, 0), (3, 0), (0, 0)])
    )
    term, term_give, up1, down1, cross, far_part, across, up_part, down_part, stay = gate(
        (term, term_give, up1, down1, cross, far_part, across, up_part, down_part, stay)
    )

    term = (term + shift(term_give, "c", 1).astype(F32)).reshape(4, 2, HD, half)
    term, term_give = term[:, 0], shift(term[:, 1].astype(BF16), "xh", 1)
    far_part = (far_part.astype(F32) + cross.astype(F32)).astype(BF16)
    low = shift(far_part[: heads // 2], "y", 1)
    high = shift(far_part[heads // 2 :], "y", -1)
    across = (across.astype(F32) + up1.astype(F32) + down1.astype(F32)).astype(BF16)
    low, high, across, up_part, down_part, stay, term, term_give = gate(
        (low, high, across, up_part, down_part, stay, term, term_give)
    )

    across = shift(across, "xh", 1)
    term = term + term_give.astype(F32)
    send = term.astype(BF16)
    low, high = low.astype(F32), high.astype(F32)
    up0, down0 = up_part.astype(F32), down_part.astype(F32)
    up0 = jnp.concatenate(
        [(up0[: heads // 2] + low).astype(BF16), up_part[heads // 2 :], send[1]], axis=0
    )
    down0 = jnp.concatenate(
        [down_part[: heads // 2], (down0[heads // 2 :] + high).astype(BF16), send[3]], axis=0
    )
    up0, down0 = shift(up0, "y", 1), shift(down0, "y", -1)
    term_far = shift(send[2], "y", 2)
    return final_grads((stay, across, up0, down0), (term[0], term_far), output_codes, value_codes)


def solution(mesh):
    fine = Mesh(mesh.devices.reshape(tuple(SIZES.values())), tuple(SIZES))
    return jax.shard_map(
        body,
        mesh=fine,
        in_specs=(
            P(ROWS, None),
            P(ROWS, HEADS_AXES),
            P(ROWS, HEADS_AXES),
            P(ROWS, HEADS_AXES),
            P(ROWS, None),
            P(ROWS, HEADS_AXES),
            P(ROWS, HEADS_AXES),
            P(HEADS_AXES, ROWS),
            P(HEADS_AXES, ROWS),
        ),
        out_specs=(
            P(HEADS_AXES, ROWS),
            P(ROWS, HEADS_AXES),
            P(HEADS_AXES, ROWS),
            P(ROWS, HEADS_AXES),
        ),
        check_vma=False,
    )
```

```python
import jax
import jax.numpy as jnp
from jax import lax
from jax.experimental import pallas as pl
from jax.experimental.pallas import tpu as pltpu
from jax.sharding import Mesh, PartitionSpec as P

HD = 128
GROUP = 128
GQ = 8
SIZES = {"xh": 2, "y": 4, "c": 2, "z": 4, "xl": 2}
ROWS = ("xh", "y", "c")
HEADS_AXES = ("z", "xl")
F32 = jnp.float32
BF16 = jnp.bfloat16
LONG = pl.CostEstimate(flops=1 << 35, bytes_accessed=1 << 24, transcendentals=0)
BRIEF = pl.CostEstimate(flops=1 << 20, bytes_accessed=1 << 16, transcendentals=0)


def shift(x, axis, step):
    n = SIZES[axis]
    return lax.ppermute(x, axis, [(i, (i + step) % n) for i in range(n)])


def dequant_rows(codes, steps):
    rows, columns = codes.shape

    def kernel(codes_ref, steps_ref, out):
        for k in range(rows // GROUP):
            group = slice(k * GROUP, (k + 1) * GROUP)
            centered = (codes_ref[group, :] - 8).astype(F32)
            out[group, :] = (centered * steps_ref[k : k + 1, :]).astype(BF16)

    return pl.pallas_call(
        kernel,
        out_shape=jax.ShapeDtypeStruct((rows, columns), BF16),
        cost_estimate=BRIEF,
    )(codes, steps)


def dequant_transposed(codes, steps):
    rows, columns = codes.shape
    block = rows // 2
    groups = block // GROUP

    def kernel(codes_ref, steps_ref, out):
        for k in range(groups):
            group = slice(k * GROUP, (k + 1) * GROUP)
            centered = (codes_ref[group, :] - 8).astype(F32)
            step = steps_ref[pl.ds(pl.program_id(0) * groups + k, 1), :]
            out[:, group] = (centered * step).astype(BF16).T

    return pl.pallas_call(
        kernel,
        out_shape=jax.ShapeDtypeStruct((columns, rows), BF16),
        grid=(rows // block,),
        in_specs=[
            pl.BlockSpec((block, columns), lambda k: (k, 0)),
            pl.BlockSpec(steps.shape, lambda k: (0, 0)),
        ],
        out_specs=pl.BlockSpec((columns, block), lambda k: (0, k)),
        cost_estimate=BRIEF,
    )(codes, steps)


def attention_probs(queries, keys, segment_ids, first, count):
    length = keys.shape[0]

    def kernel(q_ref, k_ref, down_ref, along_ref, out, allowed):
        @pl.when(pl.program_id(0) == 0)
        def _():
            key_at = lax.broadcasted_iota(jnp.int32, (length, length), 0)
            query_at = lax.broadcasted_iota(jnp.int32, (length, length), 1)
            seen = (key_at <= query_at) & (down_ref[...] == along_ref[...])
            allowed[...] = seen.astype(F32)

        scores = lax.dot_general(
            k_ref[...], q_ref[...], (((1,), (1,)), ((), ())), preferred_element_type=F32
        ) * HD ** (-0.5)
        scores = jnp.where(allowed[...] > 0.5, scores, -1e30)
        powers = jnp.exp(scores - jnp.max(scores, axis=0, keepdims=True))
        out[0] = (powers / jnp.sum(powers, axis=0, keepdims=True)).astype(BF16)

    return pl.pallas_call(
        kernel,
        out_shape=jax.ShapeDtypeStruct((count, length, length), BF16),
        grid=(count,),
        in_specs=[
            pl.BlockSpec((length, HD), lambda h: (0, first + h)),
            pl.BlockSpec((length, HD), lambda h: (0, 0)),
            pl.BlockSpec((length, 1), lambda h: (0, 0)),
            pl.BlockSpec((1, length), lambda h: (0, 0)),
        ],
        out_specs=pl.BlockSpec((1, length, length), lambda h: (h, 0, 0)),
        scratch_shapes=[pltpu.VMEM((length, length), F32)],
        compiler_params=pltpu.CompilerParams(vmem_limit_bytes=32 << 20),
        cost_estimate=LONG,
    )(queries, keys, segment_ids.reshape(length, 1), segment_ids)


def attended_heads(hidden_in, value_weight, probs):
    width, columns = value_weight.shape
    rows = hidden_in.shape[0]
    heads = 2 * probs[0].shape[0]
    count = 8
    depth = width // count

    def kernel(h_ref, v_ref, p_low, p_high, out, total):
        k = pl.program_id(0)
        more = jnp.dot(h_ref[...], v_ref[...], preferred_element_type=F32)

        @pl.when(k == 0)
        def _():
            total[...] = more

        @pl.when(k > 0)
        def _():
            total[...] += more

        @pl.when(k == count - 1)
        def _():
            values = total[...].T.astype(BF16)
            for h in range(heads):
                p_ref = (p_low, p_high)[h // (heads // 2)]
                one = jnp.dot(values, p_ref[h % (heads // 2)], preferred_element_type=F32)
                out[h * columns : (h + 1) * columns, :] = one.astype(BF16)

    whole = pl.BlockSpec(probs[0].shape, lambda k: (0, 0, 0))
    return pl.pallas_call(
        kernel,
        out_shape=jax.ShapeDtypeStruct((heads * columns, rows), BF16),
        grid=(count,),
        in_specs=[
            pl.BlockSpec((rows, depth), lambda k: (0, k)),
            pl.BlockSpec((depth, columns), lambda k: (k, 0)),
            whole,
            whole,
        ],
        out_specs=pl.BlockSpec((heads * columns, rows), lambda k: (0, 0)),
        scratch_shapes=[pltpu.VMEM((rows, columns), F32)],
        compiler_params=pltpu.CompilerParams(vmem_limit_bytes=56 << 20),
        cost_estimate=LONG,
    )(hidden_in, value_weight, *probs)


def value_terms(hidden_in, here, there, probs, own_order, other_order):
    (count,) = own_order.shape
    rows = here.shape[0]
    width = hidden_in.shape[1] // (2 * count)
    half = probs[0].shape[0]

    def kernel(own_at, other_at, h_ref, a_ref, b_ref, p_low, p_high, *refs):
        own_out, other_out, held, total, grad, sem = refs
        fetch = pltpu.make_async_copy(h_ref, held, sem)
        fetch.start()
        for h in range(2 * half):
            head = slice(h * HD, (h + 1) * HD)
            attended_grad = (a_ref[:, head] + b_ref[:, head].astype(F32)).astype(BF16)
            more = jnp.dot(
                (p_low, p_high)[h // half][h % half], attended_grad, preferred_element_type=F32
            )
            if h == 0:
                total[...] = more
            else:
                total[...] += more
        grad[...] = total[...].T.astype(BF16)
        fetch.wait()

        def one(k, carry):
            def product(at):
                block = held[:, pl.ds(pl.multiple_of(at * width, width), width)]
                return jnp.dot(grad[...], block, preferred_element_type=F32)

            own_out[k] = product(own_at[k])
            other_out[k] = product(other_at[k]).astype(BF16)
            return carry

        lax.fori_loop(0, count, one, 0)

    whole = pl.BlockSpec(memory_space=pltpu.VMEM)
    return pl.pallas_call(
        kernel,
        out_shape=(
            jax.ShapeDtypeStruct((count, HD, width), F32),
            jax.ShapeDtypeStruct((count, HD, width), BF16),
        ),
        grid_spec=pltpu.PrefetchScalarGridSpec(
            num_scalar_prefetch=2,
            in_specs=[pl.BlockSpec(memory_space=pl.ANY)] + [whole] * 4,
            out_specs=(whole, whole),
            scratch_shapes=[
                pltpu.VMEM(hidden_in.shape, BF16),
                pltpu.VMEM((rows, HD), F32),
                pltpu.VMEM((HD, rows), BF16),
                pltpu.SemaphoreType.DMA,
            ],
        ),
        compiler_params=pltpu.CompilerParams(vmem_limit_bytes=56 << 20),
        cost_estimate=BRIEF,
    )(own_order, other_order, hidden_in, here, there, *probs)


def final_grads(weight_terms, value_terms, output_codes, value_codes):
    rows, columns = output_codes.shape
    depth, width = value_codes.shape
    steps = 4
    block = rows // steps
    groups = block // GROUP
    count = len(weight_terms)

    def centered_sums(codes, total, step_out, first):
        centered = (codes - 8).astype(F32) * total
        for k in range(total.shape[0] // GROUP):
            group = centered[k * GROUP : (k + 1) * GROUP]
            step_out[pl.ds(first + k, 1), :] = jnp.sum(group, axis=0, keepdims=True)

    def kernel(*refs):
        terms, refs = refs[:count], refs[count:]
        value_refs, refs = refs[: 2 + len(value_terms)], refs[2 + len(value_terms) :]
        codes_ref, value_codes_ref, step_out, value_step_out, out, value_out = refs
        k = pl.program_id(0)
        total = terms[0][...].astype(F32)
        for ref in terms[1:]:
            total += ref[...].astype(F32)
        out[...] = total
        centered_sums(codes_ref[...], total, step_out, k * groups)

        @pl.when(k == 0)
        def _():
            value = value_refs[0][...].astype(F32)
            for ref in value_refs[1:]:
                value += ref[...].astype(F32)
            value = value.T
            value_out[...] = value
            centered_sums(value_codes_ref[...], value, value_step_out, 0)

    part = pl.BlockSpec((block, columns), lambda k: (k, 0))
    below = pl.BlockSpec((width, columns), lambda k: (rows // width, 0))

    def whole(shape):
        return pl.BlockSpec(shape, lambda k: (0,) * len(shape))

    step_shape, value_step_shape = (rows // GROUP, columns), (depth // GROUP, width)
    return pl.pallas_call(
        kernel,
        out_shape=tuple(
            jax.ShapeDtypeStruct(shape, F32)
            for shape in (step_shape, value_step_shape, output_codes.shape, value_codes.shape)
        ),
        grid=(steps,),
        in_specs=[part] * count
        + [below] * 2
        + [whole(x.shape) for x in value_terms]
        + [part, whole(value_codes.shape)],
        out_specs=(whole(step_shape), whole(value_step_shape), part, whole(value_codes.shape)),
        compiler_params=pltpu.CompilerParams(vmem_limit_bytes=32 << 20),
        cost_estimate=BRIEF,
    )(*weight_terms, *weight_terms[-2:], *value_terms, output_codes, value_codes)


def fetch_piece(which, pieces, target, sem):
    for i, piece in enumerate(pieces):

        @pl.when(which == i)
        def _():
            pltpu.make_async_copy(piece, target, sem).start()


def head_grads(grads, weights, which, use, so_far=None):
    count, numbers = len(weights), list(grads)
    (rows, depth), heads = grads[numbers[0]].shape, weights[0].shape[1]
    half = rows // 2
    last = so_far is not None

    def kernel(which_ref, use_ref, *refs):
        g_refs, refs = refs[: len(grads)], refs[len(grads) :]
        w_refs, refs = refs[:count], refs[count:]
        g_held, w_held, g_sems, w_sems = refs[-4:]
        if last:
            before, own, other, total, earlier, sem = refs[:-4]
        else:
            (total,) = refs[:-4]
        for k in range(count):

            @pl.when(use_ref[k] == 1)
            def _():
                for number, g_ref in zip(numbers, g_refs):

                    @pl.when(which_ref[k] == number)
                    def _():
                        pltpu.make_async_copy(g_ref, g_held.at[k], g_sems.at[k]).start()

                pltpu.make_async_copy(w_refs[k], w_held.at[k], w_sems.at[k]).start()

        if last:
            start = pltpu.make_async_copy(before, earlier, sem)
            start.start()
        total[...] = jnp.zeros_like(total)

        def one(k, carry):
            @pl.when(use_ref[k] == 1)
            def _():
                pltpu.make_async_copy(g_refs[0], g_held.at[k], g_sems.at[k]).wait()
                pltpu.make_async_copy(w_refs[0], w_held.at[k], w_sems.at[k]).wait()
                total[...] += jnp.dot(g_held[k], w_held[k], preferred_element_type=F32)

            return carry

        lax.fori_loop(0, count, one, 0)
        if last:
            start.wait()
            own[...] = total[:half] + earlier[:half]
            other[...] = (total[half:] + earlier[half:]).astype(BF16)

    whole = pl.BlockSpec(memory_space=pltpu.VMEM)
    anywhere = pl.BlockSpec(memory_space=pl.ANY)
    scratch = [
        pltpu.VMEM((count, rows, depth), BF16),
        pltpu.VMEM((count, depth, heads), BF16),
        pltpu.SemaphoreType.DMA((count,)),
        pltpu.SemaphoreType.DMA((count,)),
    ]
    if last:
        sums = [pltpu.VMEM((rows, heads), F32)] * 2
        scratch = sums + [pltpu.SemaphoreType.DMA] + scratch
        out_shape = (
            jax.ShapeDtypeStruct((half, heads), F32),
            jax.ShapeDtypeStruct((half, heads), BF16),
        )
    else:
        out_shape = jax.ShapeDtypeStruct((rows, heads), F32)
    return pl.pallas_call(
        kernel,
        out_shape=out_shape,
        grid_spec=pltpu.PrefetchScalarGridSpec(
            num_scalar_prefetch=2,
            in_specs=[anywhere] * (len(grads) + count + last),
            out_specs=(whole, whole) if last else whole,
            scratch_shapes=scratch,
        ),
        compiler_params=pltpu.CompilerParams(vmem_limit_bytes=52 << 20),
        cost_estimate=BRIEF,
    )(which, use, *grads.values(), *weights, *([so_far] if last else []))


def weight_parts(attended, grads, order):
    (count,) = order.shape
    rows, depth = grads[0].shape
    heads, half = attended[0].shape
    tile = 256

    def kernel(order_ref, first, second, *refs):
        g_refs, outs, refs = refs[: len(grads)], refs[len(grads) : -6], refs[-6:]
        a_held, held, done, a_sem, sems, out_sems = refs
        a_copies = [
            pltpu.make_async_copy(first, a_held.at[:, :half], a_sem.at[0]),
            pltpu.make_async_copy(second, a_held.at[:, half:], a_sem.at[1]),
        ]
        for copy in a_copies:
            copy.start()
        for k in range(count):
            fetch_piece(order_ref[k], g_refs, held.at[k], sems.at[k])
        for copy in a_copies:
            copy.wait()
        out_copies = []
        for k in range(count):
            pltpu.make_async_copy(g_refs[0], held.at[k], sems.at[k]).wait()
            for n in range(0, depth, tile):
                block = held[k, :, n : n + tile]
                one = jnp.dot(a_held[...], block, preferred_element_type=F32)
                done[k, :, n : n + tile] = one.astype(BF16)
            out_copies.append(pltpu.make_async_copy(done.at[k], outs[k], out_sems.at[k]))
            out_copies[-1].start()
        for copy in out_copies:
            copy.wait()

    anywhere = pl.BlockSpec(memory_space=pl.ANY)
    return pl.pallas_call(
        kernel,
        out_shape=(jax.ShapeDtypeStruct((heads, depth), BF16),) * count,
        grid_spec=pltpu.PrefetchScalarGridSpec(
            num_scalar_prefetch=1,
            in_specs=[anywhere] * (2 + len(grads)),
            out_specs=(anywhere,) * count,
            scratch_shapes=[
                pltpu.VMEM((heads, rows), BF16),
                pltpu.VMEM((count, rows, depth), BF16),
                pltpu.VMEM((count, heads, depth), BF16),
                pltpu.SemaphoreType.DMA((2,)),
                pltpu.SemaphoreType.DMA((count,)),
                pltpu.SemaphoreType.DMA((count,)),
            ],
        ),
        compiler_params=pltpu.CompilerParams(vmem_limit_bytes=48 << 20),
        cost_estimate=BRIEF,
    )(order, *attended, *grads)


def gate(arrays, *after):
    flat, tree = jax.tree.flatten((arrays, after))
    return jax.tree.unflatten(tree, lax.optimization_barrier(flat))[0]


def body(
    hidden_in,
    out_grad,
    queries,
    keys,
    segment_ids,
    value_codes,
    value_steps,
    output_codes,
    output_steps,
):
    xh, y, c, z, xl = (lax.axis_index(a) for a in SIZES)
    heads, half = output_codes.shape

    others = [(distance, side) for distance in range(4) for side in (0, 1)]

    def chip_at(distance, side):
        return (xh ^ side) * 4 + (y + distance) % 4

    chips = jnp.stack([chip_at(*key) for key in others]).astype(jnp.int32)
    own_order, other_order = chips * 2 + c, chips * 2 + 1 - c

    def piece_at(distance, side):
        chip = chip_at(distance, side)
        return ((chip // 2 - z) % 4) * 2 + ((chip % 2) ^ xl)

    def pieces_at(keys_of):
        return jnp.stack([piece_at(*key) for key in keys_of]).astype(jnp.int32)

    value_weight = lax.all_gather(dequant_rows(value_codes, value_steps), ROWS, axis=0, tiled=True)
    keep = lax.dynamic_slice_in_dim(out_grad, c * half, half, 1)
    give = lax.dynamic_slice_in_dim(out_grad, (1 - c) * half, half, 1)
    grads = jnp.concatenate([keep, shift(give, "c", 1)], axis=0)
    weight = dequant_transposed(output_codes, output_steps)
    grads, weight, queries = gate((grads, weight, queries))

    g, w = {(0, 0): grads}, {(0, 0): weight}
    w[3, 0], w[1, 0] = shift(weight, "y", 1), shift(weight, "y", -1)
    g[3, 0], g[1, 0] = shift(grads, "z", 1), shift(grads, "z", -1)
    g[0, 1] = shift(grads, "xl", 1)
    probs = [attention_probs(queries, keys, segment_ids, h, GQ // 2) for h in (0, GQ // 2)]
    g, w, probs = gate((g, w, probs))

    g[3, 1], g[1, 1] = shift(g[0, 1], "z", 1), shift(g[0, 1], "z", -1)
    w[0, 1] = shift(weight, "xh", 1)
    w[2, 0] = shift(w[3, 0], "y", 1)
    g, w, value_weight, probs = gate((g, w, value_weight, probs))

    w[3, 1], w[1, 1] = shift(w[0, 1], "y", 1), shift(w[0, 1], "y", -1)
    w[2, 1] = shift(w[2, 0], "xh", 1)
    g[2, 0], g[2, 1] = shift(g[3, 0], "z", 1), shift(g[1, 1], "z", -1)
    attended = attended_heads(hidden_in, value_weight, probs)

    early = [(0, 0), (1, 0), (2, 0), (3, 0), (0, 1)]
    at_hand = {2 * d + s: g[d, s] for d, s in others if d != 2}
    at_hand, early_weights, attended = gate((at_hand, [w[key] for key in early], attended))
    use = (pieces_at(early) // 2 != 2).astype(jnp.int32)
    so_far = head_grads(at_hand, early_weights, pieces_at(early), use)
    g, w, attended, probs, so_far = gate((g, w, attended, probs, so_far))

    attended = attended, shift(attended, "c", 1)
    pieces = [g[key] for key in others]
    use = jnp.stack([jnp.where(key in early, piece_at(*key) // 2 == 2, True) for key in others])
    here, there = head_grads(
        dict(enumerate(pieces)),
        [w[key] for key in others],
        pieces_at(others),
        use.astype(jnp.int32),
        so_far,
    )
    here, there, pieces, attended = gate((here, there, pieces, attended))
    there = shift(there, "c", 1)
    up1, down1, cross = weight_parts(attended, pieces, pieces_at([(1, 1), (3, 1), (2, 1)]))
    here, there, up1, down1, cross = gate((here, there, up1, down1, cross))
    up1, down1, cross = shift(up1, "y", 1), shift(down1, "y", -1), shift(cross, "xh", 1)
    term, term_give = value_terms(hidden_in, here, there, probs, own_order, other_order)
    term, term_give, attended, pieces = gate((term, term_give, attended, pieces))
    far_part, across, up_part, down_part, stay = weight_parts(
        attended, pieces, pieces_at([(2, 0), (0, 1), (1, 0), (3, 0), (0, 0)])
    )
    term, term_give, up1, down1, cross, far_part, across, up_part, down_part, stay = gate(
        (term, term_give, up1, down1, cross, far_part, across, up_part, down_part, stay)
    )

    term = (term + shift(term_give, "c", 1).astype(F32)).reshape(4, 2, HD, half)
    term, term_give = term[:, 0], shift(term[:, 1].astype(BF16), "xh", 1)
    far_part = (far_part.astype(F32) + cross.astype(F32)).astype(BF16)
    low = shift(far_part[: heads // 2], "y", 1)
    high = shift(far_part[heads // 2 :], "y", -1)
    across = (across.astype(F32) + up1.astype(F32) + down1.astype(F32)).astype(BF16)
    low, high, across, up_part, down_part, stay, term, term_give = gate(
        (low, high, across, up_part, down_part, stay, term, term_give)
    )

    across = shift(across, "xh", 1)
    term = term + term_give.astype(F32)
    send = term.astype(BF16)
    low, high = low.astype(F32), high.astype(F32)
    up0, down0 = up_part.astype(F32), down_part.astype(F32)
    up0 = jnp.concatenate(
        [(up0[: heads // 2] + low).astype(BF16), up_part[heads // 2 :], send[1]], axis=0
    )
    down0 = jnp.concatenate(
        [down_part[: heads // 2], (down0[heads // 2 :] + high).astype(BF16), send[3]], axis=0
    )
    up0, down0 = shift(up0, "y", 1), shift(down0, "y", -1)
    term_far = shift(send[2], "y", 2)
    return final_grads((stay, across, up0, down0), (term[0], term_far), output_codes, value_codes)


def solution(mesh):
    fine = Mesh(mesh.devices.reshape(tuple(SIZES.values())), tuple(SIZES))
    return jax.shard_map(
        body,
        mesh=fine,
        in_specs=(
            P(ROWS, None),
            P(ROWS, HEADS_AXES),
            P(ROWS, HEADS_AXES),
            P(ROWS, HEADS_AXES),
            P(ROWS, None),
            P(ROWS, HEADS_AXES),
            P(ROWS, HEADS_AXES),
            P(HEADS_AXES, ROWS),
            P(HEADS_AXES, ROWS),
        ),
        out_specs=(
            P(HEADS_AXES, ROWS),
            P(ROWS, HEADS_AXES),
            P(HEADS_AXES, ROWS),
            P(ROWS, HEADS_AXES),
        ),
        check_vma=False,
    )
```

```python
import jax
import jax.numpy as jnp
from jax import lax
from jax.experimental import pallas as pl
from jax.experimental.pallas import tpu as pltpu
from jax.sharding import Mesh, PartitionSpec as P

HD = 128
GROUP = 128
GQ = 8
SIZES = {"xh": 2, "y": 4, "c": 2, "z": 4, "xl": 2}
ROWS = ("xh", "y", "c")
HEADS_AXES = ("z", "xl")
F32 = jnp.float32
BF16 = jnp.bfloat16
LONG = pl.CostEstimate(flops=1 << 35, bytes_accessed=1 << 24, transcendentals=0)
BRIEF = pl.CostEstimate(flops=1 << 20, bytes_accessed=1 << 16, transcendentals=0)


def shift(x, axis, step):
    n = SIZES[axis]
    return lax.ppermute(x, axis, [(i, (i + step) % n) for i in range(n)])


def dequant_rows(codes, steps):
    rows, columns = codes.shape

    def kernel(codes_ref, steps_ref, out):
        for k in range(rows // GROUP):
            group = slice(k * GROUP, (k + 1) * GROUP)
            centered = (codes_ref[group, :] - 8).astype(F32)
            out[group, :] = (centered * steps_ref[k : k + 1, :]).astype(BF16)

    return pl.pallas_call(
        kernel,
        out_shape=jax.ShapeDtypeStruct((rows, columns), BF16),
        cost_estimate=BRIEF,
    )(codes, steps)


def dequant_transposed(codes, steps):
    rows, columns = codes.shape
    block = rows // 2
    groups = block // GROUP

    def kernel(codes_ref, steps_ref, out):
        for k in range(groups):
            group = slice(k * GROUP, (k + 1) * GROUP)
            centered = (codes_ref[group, :] - 8).astype(F32)
            step = steps_ref[pl.ds(pl.program_id(0) * groups + k, 1), :]
            out[:, group] = (centered * step).astype(BF16).T

    return pl.pallas_call(
        kernel,
        out_shape=jax.ShapeDtypeStruct((columns, rows), BF16),
        grid=(rows // block,),
        in_specs=[
            pl.BlockSpec((block, columns), lambda k: (k, 0)),
            pl.BlockSpec(steps.shape, lambda k: (0, 0)),
        ],
        out_specs=pl.BlockSpec((columns, block), lambda k: (0, k)),
        cost_estimate=BRIEF,
    )(codes, steps)


def attention_probs(queries, keys, segment_ids, first, count):
    length = keys.shape[0]

    def kernel(q_ref, k_ref, down_ref, along_ref, out, allowed):
        @pl.when(pl.program_id(0) == 0)
        def _():
            key_at = lax.broadcasted_iota(jnp.int32, (length, length), 0)
            query_at = lax.broadcasted_iota(jnp.int32, (length, length), 1)
            seen = (key_at <= query_at) & (down_ref[...] == along_ref[...])
            allowed[...] = seen.astype(F32)

        scores = lax.dot_general(
            k_ref[...], q_ref[...], (((1,), (1,)), ((), ())), preferred_element_type=F32
        ) * HD ** (-0.5)
        scores = jnp.where(allowed[...] > 0.5, scores, -1e30)
        powers = jnp.exp(scores - jnp.max(scores, axis=0, keepdims=True))
        out[0] = (powers / jnp.sum(powers, axis=0, keepdims=True)).astype(BF16)

    return pl.pallas_call(
        kernel,
        out_shape=jax.ShapeDtypeStruct((count, length, length), BF16),
        grid=(count,),
        in_specs=[
            pl.BlockSpec((length, HD), lambda h: (0, first + h)),
            pl.BlockSpec((length, HD), lambda h: (0, 0)),
            pl.BlockSpec((length, 1), lambda h: (0, 0)),
            pl.BlockSpec((1, length), lambda h: (0, 0)),
        ],
        out_specs=pl.BlockSpec((1, length, length), lambda h: (h, 0, 0)),
        scratch_shapes=[pltpu.VMEM((length, length), F32)],
        compiler_params=pltpu.CompilerParams(vmem_limit_bytes=32 << 20),
        cost_estimate=LONG,
    )(queries, keys, segment_ids.reshape(length, 1), segment_ids)


def attended_heads(hidden_in, value_weight, probs):
    width, columns = value_weight.shape
    rows = hidden_in.shape[0]
    heads = 2 * probs[0].shape[0]
    count = 8
    depth = width // count

    def kernel(h_ref, v_ref, p_low, p_high, out, total):
        k = pl.program_id(0)
        more = jnp.dot(h_ref[...], v_ref[...], preferred_element_type=F32)

        @pl.when(k == 0)
        def _():
            total[...] = more

        @pl.when(k > 0)
        def _():
            total[...] += more

        @pl.when(k == count - 1)
        def _():
            values = total[...].T.astype(BF16)
            for h in range(heads):
                p_ref = (p_low, p_high)[h // (heads // 2)]
                one = jnp.dot(values, p_ref[h % (heads // 2)], preferred_element_type=F32)
                out[h * columns : (h + 1) * columns, :] = one.astype(BF16)

    whole = pl.BlockSpec(probs[0].shape, lambda k: (0, 0, 0))
    return pl.pallas_call(
        kernel,
        out_shape=jax.ShapeDtypeStruct((heads * columns, rows), BF16),
        grid=(count,),
        in_specs=[
            pl.BlockSpec((rows, depth), lambda k: (0, k)),
            pl.BlockSpec((depth, columns), lambda k: (k, 0)),
            whole,
            whole,
        ],
        out_specs=pl.BlockSpec((heads * columns, rows), lambda k: (0, 0)),
        scratch_shapes=[pltpu.VMEM((rows, columns), F32)],
        compiler_params=pltpu.CompilerParams(vmem_limit_bytes=56 << 20),
        cost_estimate=LONG,
    )(hidden_in, value_weight, *probs)


def value_terms(hidden_in, here, there, probs, own_order, other_order):
    (count,) = own_order.shape
    rows = here.shape[0]
    width = hidden_in.shape[1] // (2 * count)
    half = probs[0].shape[0]

    def kernel(own_at, other_at, h_ref, a_ref, b_ref, p_low, p_high, *refs):
        own_out, other_out, held, total, grad, sem = refs
        fetch = pltpu.make_async_copy(h_ref, held, sem)
        fetch.start()
        for h in range(2 * half):
            head = slice(h * HD, (h + 1) * HD)
            attended_grad = (
                a_ref[:, head].astype(F32) + b_ref[:, head].astype(F32)
            ).astype(BF16)
            more = jnp.dot(
                (p_low, p_high)[h // half][h % half], attended_grad, preferred_element_type=F32
            )
            if h == 0:
                total[...] = more
            else:
                total[...] += more
        grad[...] = total[...].T.astype(BF16)
        fetch.wait()

        def one(k, carry):
            def product(at):
                block = held[:, pl.ds(pl.multiple_of(at * width, width), width)]
                return jnp.dot(grad[...], block, preferred_element_type=F32)

            own_out[k] = product(own_at[k])
            other_out[k] = product(other_at[k]).astype(BF16)
            return carry

        lax.fori_loop(0, count, one, 0)

    whole = pl.BlockSpec(memory_space=pltpu.VMEM)
    return pl.pallas_call(
        kernel,
        out_shape=(
            jax.ShapeDtypeStruct((count, HD, width), F32),
            jax.ShapeDtypeStruct((count, HD, width), BF16),
        ),
        grid_spec=pltpu.PrefetchScalarGridSpec(
            num_scalar_prefetch=2,
            in_specs=[pl.BlockSpec(memory_space=pl.ANY)] + [whole] * 4,
            out_specs=(whole, whole),
            scratch_shapes=[
                pltpu.VMEM(hidden_in.shape, BF16),
                pltpu.VMEM((rows, HD), F32),
                pltpu.VMEM((HD, rows), BF16),
                pltpu.SemaphoreType.DMA,
            ],
        ),
        compiler_params=pltpu.CompilerParams(vmem_limit_bytes=56 << 20),
        cost_estimate=BRIEF,
    )(own_order, other_order, hidden_in, here, there, *probs)


def final_grads(weight_terms, value_terms, output_codes, value_codes):
    rows, columns = output_codes.shape
    depth, width = value_codes.shape
    steps = 4
    block = rows // steps
    groups = block // GROUP
    count = len(weight_terms)

    def centered_sums(codes, total, step_out, first):
        centered = (codes - 8).astype(F32) * total
        for k in range(total.shape[0] // GROUP):
            group = centered[k * GROUP : (k + 1) * GROUP]
            step_out[pl.ds(first + k, 1), :] = jnp.sum(group, axis=0, keepdims=True)

    def kernel(*refs):
        terms, refs = refs[:count], refs[count:]
        value_refs, refs = refs[: 2 + len(value_terms)], refs[2 + len(value_terms) :]
        codes_ref, value_codes_ref, step_out, value_step_out, out, value_out = refs
        k = pl.program_id(0)
        total = terms[0][...].astype(F32)
        for ref in terms[1:]:
            total += ref[...].astype(F32)
        out[...] = total
        centered_sums(codes_ref[...], total, step_out, k * groups)

        @pl.when(k == 0)
        def _():
            value = value_refs[0][...].astype(F32)
            for ref in value_refs[1:]:
                value += ref[...].astype(F32)
            value = value.T
            value_out[...] = value
            centered_sums(value_codes_ref[...], value, value_step_out, 0)

    part = pl.BlockSpec((block, columns), lambda k: (k, 0))
    below = pl.BlockSpec((width, columns), lambda k: (rows // width, 0))

    def whole(shape):
        return pl.BlockSpec(shape, lambda k: (0,) * len(shape))

    step_shape, value_step_shape = (rows // GROUP, columns), (depth // GROUP, width)
    return pl.pallas_call(
        kernel,
        out_shape=tuple(
            jax.ShapeDtypeStruct(shape, F32)
            for shape in (step_shape, value_step_shape, output_codes.shape, value_codes.shape)
        ),
        grid=(steps,),
        in_specs=[part] * count
        + [below] * 2
        + [whole(x.shape) for x in value_terms]
        + [part, whole(value_codes.shape)],
        out_specs=(whole(step_shape), whole(value_step_shape), part, whole(value_codes.shape)),
        compiler_params=pltpu.CompilerParams(vmem_limit_bytes=32 << 20),
        cost_estimate=BRIEF,
    )(*weight_terms, *weight_terms[-2:], *value_terms, output_codes, value_codes)


def fetch_piece(which, pieces, target, sem):
    for i, piece in enumerate(pieces):

        @pl.when(which == i)
        def _():
            pltpu.make_async_copy(piece, target, sem).start()


def head_grads(grads, weights, which, use, so_far=None):
    count, numbers = len(weights), list(grads)
    (rows, depth), heads = grads[numbers[0]].shape, weights[0].shape[1]
    half = rows // 2
    last = so_far is not None

    def kernel(which_ref, use_ref, *refs):
        g_refs, refs = refs[: len(grads)], refs[len(grads) :]
        w_refs, refs = refs[:count], refs[count:]
        g_held, w_held, g_sems, w_sems = refs[-4:]
        if last:
            before, own, other, total, earlier, sem = refs[:-4]
        else:
            (total,) = refs[:-4]
        for k in range(count):

            @pl.when(use_ref[k] == 1)
            def _():
                for number, g_ref in zip(numbers, g_refs):

                    @pl.when(which_ref[k] == number)
                    def _():
                        pltpu.make_async_copy(g_ref, g_held.at[k], g_sems.at[k]).start()

                pltpu.make_async_copy(w_refs[k], w_held.at[k], w_sems.at[k]).start()

        if last:
            start = pltpu.make_async_copy(before, earlier, sem)
            start.start()
        total[...] = jnp.zeros_like(total)

        def one(k, carry):
            @pl.when(use_ref[k] == 1)
            def _():
                pltpu.make_async_copy(g_refs[0], g_held.at[k], g_sems.at[k]).wait()
                pltpu.make_async_copy(w_refs[0], w_held.at[k], w_sems.at[k]).wait()
                total[...] += jnp.dot(g_held[k], w_held[k], preferred_element_type=F32)

            return carry

        lax.fori_loop(0, count, one, 0)
        if last:
            start.wait()
            own[...] = (total[:half] + earlier[:half]).astype(BF16)
            other[...] = (total[half:] + earlier[half:]).astype(BF16)

    whole = pl.BlockSpec(memory_space=pltpu.VMEM)
    anywhere = pl.BlockSpec(memory_space=pl.ANY)
    scratch = [
        pltpu.VMEM((count, rows, depth), BF16),
        pltpu.VMEM((count, depth, heads), BF16),
        pltpu.SemaphoreType.DMA((count,)),
        pltpu.SemaphoreType.DMA((count,)),
    ]
    if last:
        sums = [pltpu.VMEM((rows, heads), F32)] * 2
        scratch = sums + [pltpu.SemaphoreType.DMA] + scratch
        out_shape = (jax.ShapeDtypeStruct((half, heads), BF16),) * 2
    else:
        out_shape = jax.ShapeDtypeStruct((rows, heads), F32)
    return pl.pallas_call(
        kernel,
        out_shape=out_shape,
        grid_spec=pltpu.PrefetchScalarGridSpec(
            num_scalar_prefetch=2,
            in_specs=[anywhere] * (len(grads) + count + last),
            out_specs=(whole, whole) if last else whole,
            scratch_shapes=scratch,
        ),
        compiler_params=pltpu.CompilerParams(vmem_limit_bytes=52 << 20),
        cost_estimate=BRIEF,
    )(which, use, *grads.values(), *weights, *([so_far] if last else []))


def weight_parts(attended, grads, order):
    (count,) = order.shape
    rows, depth = grads[0].shape
    heads, half = attended[0].shape
    tile = 256

    def kernel(order_ref, first, second, *refs):
        g_refs, outs, refs = refs[: len(grads)], refs[len(grads) : -6], refs[-6:]
        a_held, held, done, a_sem, sems, out_sems = refs
        a_copies = [
            pltpu.make_async_copy(first, a_held.at[:, :half], a_sem.at[0]),
            pltpu.make_async_copy(second, a_held.at[:, half:], a_sem.at[1]),
        ]
        for copy in a_copies:
            copy.start()
        for k in range(count):
            fetch_piece(order_ref[k], g_refs, held.at[k], sems.at[k])
        for copy in a_copies:
            copy.wait()
        out_copies = []
        for k in range(count):
            pltpu.make_async_copy(g_refs[0], held.at[k], sems.at[k]).wait()
            for n in range(0, depth, tile):
                block = held[k, :, n : n + tile]
                one = jnp.dot(a_held[...], block, preferred_element_type=F32)
                done[k, :, n : n + tile] = one.astype(BF16)
            out_copies.append(pltpu.make_async_copy(done.at[k], outs[k], out_sems.at[k]))
            out_copies[-1].start()
        for copy in out_copies:
            copy.wait()

    anywhere = pl.BlockSpec(memory_space=pl.ANY)
    return pl.pallas_call(
        kernel,
        out_shape=(jax.ShapeDtypeStruct((heads, depth), BF16),) * count,
        grid_spec=pltpu.PrefetchScalarGridSpec(
            num_scalar_prefetch=1,
            in_specs=[anywhere] * (2 + len(grads)),
            out_specs=(anywhere,) * count,
            scratch_shapes=[
                pltpu.VMEM((heads, rows), BF16),
                pltpu.VMEM((count, rows, depth), BF16),
                pltpu.VMEM((count, heads, depth), BF16),
                pltpu.SemaphoreType.DMA((2,)),
                pltpu.SemaphoreType.DMA((count,)),
                pltpu.SemaphoreType.DMA((count,)),
            ],
        ),
        compiler_params=pltpu.CompilerParams(vmem_limit_bytes=48 << 20),
        cost_estimate=BRIEF,
    )(order, *attended, *grads)


def gate(arrays, *after):
    flat, tree = jax.tree.flatten((arrays, after))
    return jax.tree.unflatten(tree, lax.optimization_barrier(flat))[0]


def body(
    hidden_in,
    out_grad,
    queries,
    keys,
    segment_ids,
    value_codes,
    value_steps,
    output_codes,
    output_steps,
):
    xh, y, c, z, xl = (lax.axis_index(a) for a in SIZES)
    heads, half = output_codes.shape

    others = [(distance, side) for distance in range(4) for side in (0, 1)]

    def chip_at(distance, side):
        return (xh ^ side) * 4 + (y + distance) % 4

    chips = jnp.stack([chip_at(*key) for key in others]).astype(jnp.int32)
    own_order, other_order = chips * 2 + c, chips * 2 + 1 - c

    def piece_at(distance, side):
        chip = chip_at(distance, side)
        return ((chip // 2 - z) % 4) * 2 + ((chip % 2) ^ xl)

    def pieces_at(keys_of):
        return jnp.stack([piece_at(*key) for key in keys_of]).astype(jnp.int32)

    value_weight = lax.all_gather(dequant_rows(value_codes, value_steps), ROWS, axis=0, tiled=True)
    keep = lax.dynamic_slice_in_dim(out_grad, c * half, half, 1)
    give = lax.dynamic_slice_in_dim(out_grad, (1 - c) * half, half, 1)
    grads = jnp.concatenate([keep, shift(give, "c", 1)], axis=0)
    weight = dequant_transposed(output_codes, output_steps)
    grads, weight, queries = gate((grads, weight, queries))

    g, w = {(0, 0): grads}, {(0, 0): weight}
    w[3, 0], w[1, 0] = shift(weight, "y", 1), shift(weight, "y", -1)
    g[3, 0], g[1, 0] = shift(grads, "z", 1), shift(grads, "z", -1)
    g[0, 1] = shift(grads, "xl", 1)
    probs = [attention_probs(queries, keys, segment_ids, h, GQ // 2) for h in (0, GQ // 2)]
    g, w, probs = gate((g, w, probs))

    g[3, 1], g[1, 1] = shift(g[0, 1], "z", 1), shift(g[0, 1], "z", -1)
    w[0, 1] = shift(weight, "xh", 1)
    w[2, 0] = shift(w[3, 0], "y", 1)
    g, w, value_weight, probs = gate((g, w, value_weight, probs))

    w[3, 1], w[1, 1] = shift(w[0, 1], "y", 1), shift(w[0, 1], "y", -1)
    w[2, 1] = shift(w[2, 0], "xh", 1)
    g[2, 0], g[2, 1] = shift(g[3, 0], "z", 1), shift(g[1, 1], "z", -1)
    attended = attended_heads(hidden_in, value_weight, probs)

    early = [(0, 0), (1, 0), (2, 0), (3, 0), (0, 1)]
    at_hand = {2 * d + s: g[d, s] for d, s in others if d != 2}
    at_hand, early_weights, attended = gate((at_hand, [w[key] for key in early], attended))
    use = (pieces_at(early) // 2 != 2).astype(jnp.int32)
    so_far = head_grads(at_hand, early_weights, pieces_at(early), use)
    g, w, attended, probs, so_far = gate((g, w, attended, probs, so_far))

    attended = attended, shift(attended, "c", 1)
    pieces = [g[key] for key in others]
    use = jnp.stack([jnp.where(key in early, piece_at(*key) // 2 == 2, True) for key in others])
    here, there = head_grads(
        dict(enumerate(pieces)),
        [w[key] for key in others],
        pieces_at(others),
        use.astype(jnp.int32),
        so_far,
    )
    here, there, pieces, attended = gate((here, there, pieces, attended))
    there = shift(there, "c", 1)
    up1, down1, cross = weight_parts(attended, pieces, pieces_at([(1, 1), (3, 1), (2, 1)]))
    here, there, up1, down1, cross = gate((here, there, up1, down1, cross))
    up1, down1, cross = shift(up1, "y", 1), shift(down1, "y", -1), shift(cross, "xh", 1)
    term, term_give = value_terms(hidden_in, here, there, probs, own_order, other_order)
    term, term_give, attended, pieces = gate((term, term_give, attended, pieces))
    far_part, across, up_part, down_part, stay = weight_parts(
        attended, pieces, pieces_at([(2, 0), (0, 1), (1, 0), (3, 0), (0, 0)])
    )
    term, term_give, up1, down1, cross, far_part, across, up_part, down_part, stay = gate(
        (term, term_give, up1, down1, cross, far_part, across, up_part, down_part, stay)
    )

    term = (term + shift(term_give, "c", 1).astype(F32)).reshape(4, 2, HD, half)
    term, term_give = term[:, 0], shift(term[:, 1].astype(BF16), "xh", 1)
    far_part = (far_part.astype(F32) + cross.astype(F32)).astype(BF16)
    low = shift(far_part[: heads // 2], "y", 1)
    high = shift(far_part[heads // 2 :], "y", -1)
    across = (across.astype(F32) + up1.astype(F32) + down1.astype(F32)).astype(BF16)
    low, high, across, up_part, down_part, stay, term, term_give = gate(
        (low, high, across, up_part, down_part, stay, term, term_give)
    )

    across = shift(across, "xh", 1)
    term = term + term_give.astype(F32)
    send = term.astype(BF16)
    low, high = low.astype(F32), high.astype(F32)
    up0, down0 = up_part.astype(F32), down_part.astype(F32)
    up0 = jnp.concatenate(
        [(up0[: heads // 2] + low).astype(BF16), up_part[heads // 2 :], send[1]], axis=0
    )
    down0 = jnp.concatenate(
        [down_part[: heads // 2], (down0[heads // 2 :] + high).astype(BF16), send[3]], axis=0
    )
    up0, down0 = shift(up0, "y", 1), shift(down0, "y", -1)
    term_far = shift(send[2], "y", 2)
    return final_grads((stay, across, up0, down0), (term[0], term_far), output_codes, value_codes)


def solution(mesh):
    fine = Mesh(mesh.devices.reshape(tuple(SIZES.values())), tuple(SIZES))
    return jax.shard_map(
        body,
        mesh=fine,
        in_specs=(
            P(ROWS, None),
            P(ROWS, HEADS_AXES),
            P(ROWS, HEADS_AXES),
            P(ROWS, HEADS_AXES),
            P(ROWS, None),
            P(ROWS, HEADS_AXES),
            P(ROWS, HEADS_AXES),
            P(HEADS_AXES, ROWS),
            P(HEADS_AXES, ROWS),
        ),
        out_specs=(
            P(HEADS_AXES, ROWS),
            P(ROWS, HEADS_AXES),
            P(HEADS_AXES, ROWS),
            P(ROWS, HEADS_AXES),
        ),
        check_vma=False,
    )
```
